256 devices in a mesh: row: 16 (over y, x), col: 16 (over z, core).
Axes of the slice: x: 4, y: 4, z: 8, core: 2. Of those that a mesh axis runs over, the one named last changes fastest.
Arguments:
- points: float32 [3, 32768], P(None, ('row', 'col')), may hold values from -0.03 to 8, as said below
- amplitude: float32 [32768], P(('row', 'col')), may hold values from 0.5 to 2
- sketch: bfloat16 [32768, 512], P(('row', 'col')), may hold values from -6 to 6
Outputs:
- kl_modes: float32 [32768, 512], P(('row', 'col'))
The draws below stay inside these ranges and needn't reach their ends.
Inputs may be any that keep to these rules, and one draw needn't show every extreme that they name: `points`: each point lies near a lattice site of spacing 1/16, sixteen sites along x and y.
All inputs are finite; a program needn't handle non-finite values.
Results may differ from the reference program's by a relative error of at most 0.0003.
The reference program's roundings to bfloat16 on the way count: a program that leaves them out, or rounds other values in their place, can miss the bound.
Values may be sent and summed in bfloat16 or wider, within the bound.
A program may use at most 64 MiB of HBM per device.

```python
import math
import jax
import jax.numpy as jnp
from jax import lax

RANK = 512
PTS_DEV = 128
NS_ITERS = 3
NPTS = 32768
N_ROW = 16
N_COL = 16


def draw_points(key, part):
    point_index = jnp.arange(NPTS, dtype=jnp.int32)
    lattice = jnp.stack([point_index % 16, point_index // 16 % 16, point_index // 256]).astype(jnp.float32)
    jitter = jnp.clip(0.15 * jax.random.normal(key, (3, NPTS), jnp.float32), -0.45, 0.45)
    return (lattice + jitter) / 16.0


def levels(own_key, shape, pieces, smallest, largest):
    factor_of = 1.0
    for position, blocks in pieces:
        steps = jax.random.uniform(jax.random.fold_in(jax.random.fold_in(own_key, 6), position), (blocks,), jnp.float32, smallest / len(pieces), largest / len(pieces))
        factor_of = factor_of * jnp.repeat(jnp.exp(steps), shape[position] // blocks).reshape((-1,) + (1,) * (len(shape) - 1 - position))
    return factor_of


def scatter_about(own_key, shape, scale, bound, shards=(), held_as=jnp.bfloat16):
    entries = scale * jax.random.normal(own_key, shape, jnp.float32)
    if shards:
        entries = entries * levels(own_key, shape, shards, -0.22, 0.18)
    return jnp.clip(entries, -bound, bound).astype(held_as)


def setup_inputs(seed: int = 0) -> dict:
    key_list = jax.random.split(jax.random.key(seed), 4)
    return {
        "points": draw_points(jax.random.fold_in(key_list[3], 71), 0),
        "amplitude": jnp.clip(jnp.exp(math.log(2.0) - 1.3862944 * jax.random.uniform(key_list[1], (NPTS,), jnp.float32) ** levels(key_list[1], (NPTS,), ((0, 256),), -0.2, 0.2)), 0.5, 2.0),
        "sketch": scatter_about(key_list[2], (NPTS, RANK), 1.0, 6.0, ((0, 256),)),
    }


correlation = 4.0

def kernel_tile(row_pts, row_amp, row_index, col_pts, col_amp, col_index, weight):
    distance = jnp.zeros((row_pts.shape[1], col_pts.shape[1]), jnp.float32)
    for component in range(3):
        offset = row_pts[component][:, None] - col_pts[component][None, :]
        distance = distance + offset * offset
    covariance = weight * row_amp[:, None] * col_amp[None, :] * jnp.exp(-jnp.sqrt(distance) / correlation)
    covariance = covariance + (row_index[:, None] == col_index[None, :]).astype(jnp.float32)
    return covariance.astype(jnp.bfloat16)

def reference(points, amplitude, sketch):
    highest = lax.Precision.HIGHEST
    point_total = points.shape[1]
    weight = 0.5 / math.sqrt(point_total)
    span = PTS_DEV * N_COL
    all_index = jnp.arange(point_total, dtype=jnp.int32)

    def one_block(block_start):
        row_pts = lax.dynamic_slice_in_dim(points, block_start, span, 1)
        row_amp = lax.dynamic_slice_in_dim(amplitude, block_start, span, 0)
        row_index = block_start + jnp.arange(span, dtype=jnp.int32)
        kernel_block = kernel_tile(row_pts, row_amp, row_index, points, amplitude, all_index, weight)
        return jnp.dot(kernel_block, sketch, preferred_element_type=jnp.float32)
    starts = jnp.arange(N_ROW, dtype=jnp.int32) * span
    sketched = lax.map(one_block, starts).reshape(point_total, RANK)
    gram_matrix = jnp.dot(sketched.T, sketched, precision=highest)
    norm_gram = jnp.sqrt(jnp.sum(gram_matrix * gram_matrix))
    iterate = gram_matrix / norm_gram
    identity = jnp.eye(RANK, dtype=jnp.float32)
    partner = identity
    for newton_step in range(NS_ITERS):
        middle = 1.5 * identity - 0.5 * jnp.dot(partner, iterate, precision=highest)
        iterate, partner = (jnp.dot(iterate, middle, precision=highest), jnp.dot(middle, partner, precision=highest))
    rotation = partner / jnp.sqrt(norm_gram)
    return math.sqrt(RANK) * jnp.dot(sketched, rotation, precision=highest)
```

```python
import math

import jax
import jax.numpy as jnp
from jax import lax
from jax.experimental import pallas as pl
from jax.experimental.pallas import tpu as pltpu
from jax.sharding import PartitionSpec as P

NS_ITERS = 3
CORRELATION = 4.0

MESH = pl.DeviceIdType.MESH
NX, NY, NZ, NCORE = 4, 4, 8, 2
PTS = 128
RANK = 512
WIDTH = 256
PARTS = RANK // WIDTH
ROWS = NZ * PTS
COLS = NX * NY * NCORE * PTS
FEATS = 48
OFFSETS = (4, 3, -3, 2, -2, 1, -1, 0)
SLOT = {off: i for i, off in enumerate(OFFSETS)}
UP = ((4, 0), (3, 1), (3, 0), (2, 1), (2, 0), (1, 1), (1, 0))
DOWN = ((4, 1), (-3, 0), (-3, 1), (-2, 0), (-2, 1), (-1, 0), (-1, 1))
BLOCKS = (
    ((0, 0), (0, 1), (0, 2), (0, 3), (1, 1)),
    ((1, 2), (1, 3), (2, 2), (2, 3), (3, 3)),
)
PLANE = tuple((dy, dx) for dy in range(NY) for dx in range(NX) if (dy, dx) != (0, 0))


def three_parts(v):
    high = v.astype(jnp.bfloat16).astype(jnp.float32)
    rest = v - high
    mid = rest.astype(jnp.bfloat16).astype(jnp.float32)
    low = (rest - mid).astype(jnp.bfloat16).astype(jnp.float32)
    return high, mid, low


def kernel(
    points,
    amplitude,
    sketch,
    out,
    row_pack,
    col_pack,
    row_packs,
    col_packs,
    row_feats,
    row_level,
    col_feats,
    col_level,
    tile,
    stripe,
    partial,
    up_in,
    down_in,
    basis,
    gram_part,
    plane_in,
    plane_sum,
    line_in,
    line_sum,
    gram_half,
    gram,
    square,
    polynomial,
    pack_sems,
    stripe_sems,
    ring_sems,
    basis_sems,
    gram_sems,
):
    row = lax.axis_index("row")
    col = lax.axis_index("col")
    y, x = lax.div(row, NX), lax.rem(row, NX)
    z, core = lax.div(col, NCORE), lax.rem(col, NCORE)

    def device(dy=0, dx=0, dz=0, dcore=0):
        return (
            lax.rem(y + dy + NY, NY) * NX + lax.rem(x + dx + NX, NX),
            lax.rem(z + dz + NZ, NZ) * NCORE + lax.rem(core + dcore, NCORE),
        )

    def send(src, dst, sems, index, to):
        copy = pltpu.make_async_remote_copy(
            src_ref=src,
            dst_ref=dst,
            send_sem=sems.at[0, index],
            recv_sem=sems.at[1, index],
            device_id=to,
            device_id_type=MESH,
        )
        copy.start()
        started.append(copy)
        return copy

    started = []
    other = device(dcore=1)

    barrier = pltpu.get_barrier_semaphore()
    for dy, dx in PLANE:
        pl.semaphore_signal(barrier, inc=1, device_id=device(dy=dy, dx=dx), device_id_type=MESH)
    for dz in range(1, NZ):
        pl.semaphore_signal(barrier, inc=1, device_id=device(dz=dz), device_id_type=MESH)
    pl.semaphore_signal(barrier, inc=1, device_id=other, device_id_type=MESH)

    weight = 0.5 / math.sqrt(ROWS * NX * NY * NCORE)
    per_unit = 1.0 / (CORRELATION * math.log(2.0))
    amp = amplitude[...]
    level = jnp.log(amp) * (1.0 / math.log(2.0)) + 0.5 * math.log2(weight)
    ux = (points[0:1, :] - 0.5) * per_unit
    uy = (points[1:2, :] - 0.5) * per_unit
    uz = (points[2:3, :] - 4.0) * per_unit
    norm = ux * ux + uy * uy + uz * uz
    row_pack[...] = jnp.zeros_like(row_pack)
    col_pack[...] = jnp.zeros_like(col_pack)
    for i, v in enumerate((ux, uy, uz)):
        row_pack[i : i + 1, :] = v
        col_pack[i : i + 1, :] = -2.0 * v
    row_pack[3:4, :] = norm
    row_pack[4:5, :] = jnp.ones_like(norm)
    row_pack[5:6, :] = level
    col_pack[3:4, :] = jnp.ones_like(norm)
    col_pack[4:5, :] = norm
    col_pack[6:7, :] = level
    row_packs[SLOT[0]] = row_pack[...]
    col_packs[0, 0, 0] = col_pack[...]
    for t in range(4):
        stripe[t, 0, 0, 0] = sketch[:, t * 128 : (t + 1) * 128]

    pl.semaphore_wait(barrier, len(PLANE) + NZ)

    line_packs = []
    for dz in range(1, NZ):
        at = SLOT[-dz if dz <= 3 else 8 - dz]
        line_packs.append(
            send(row_pack, row_packs.at[at], pack_sems, at, device(dz=dz))
        )
    plane_packs = []
    for dy, dx in PLANE:
        at = (-dy % NY, -dx % NX)
        plane_packs.append(
            send(
                col_pack,
                col_packs.at[0, at[0], at[1]],
                pack_sems,
                8 + at[0] * NX + at[1],
                device(dy=dy, dx=dx),
            )
        )
    first = {}
    for t in range(4):
        first[t] = []
        for d in range(1, 4):
            if t % 2 == 0:
                dst, to = stripe.at[t, 0, 0, -d % NX], device(dx=d)
            else:
                dst, to = stripe.at[t, 0, -d % NY, 0], device(dy=d)
            src = sketch.at[:, t * 128 : (t + 1) * 128]
            first[t].append(send(src, dst, stripe_sems, t * 8 + d, to))
    for copy in plane_packs:
        copy.wait_recv()
    pack_share = send(col_packs.at[0], col_packs.at[1], pack_sems, 8, other)
    second = {}
    for t in range(4):
        for copy in first[t]:
            copy.wait_recv()
        second[t] = []
        for d in range(1, 4):
            if t % 2 == 0:
                src, dst, to = stripe.at[t, 0, 0], stripe.at[t, 0, -d % NY], device(dy=d)
            else:
                src, dst, to = (
                    stripe.at[t, 0, :, 0],
                    stripe.at[t, 0, :, -d % NX],
                    device(dx=d),
                )
            second[t].append(send(src, dst, stripe_sems, t * 8 + 3 + d, to))
    for copy in line_packs:
        copy.wait_recv()

    def row_side(i, carry):
        pack = row_packs[i]
        high, mid, low = three_parts(pack)
        feats = jnp.concatenate([high, high, mid, high, low, mid], axis=0)
        feats = jnp.concatenate([feats, jnp.zeros((128 - FEATS, PTS), jnp.float32)], axis=0)
        at = pl.multiple_of(i * PTS, PTS)
        row_feats[pl.ds(at, PTS), :] = feats.T.astype(jnp.bfloat16)
        row_level[pl.ds(at, PTS), :] = jnp.broadcast_to(pack[5:6, :], (PTS, PTS)).T
        return carry

    lax.fori_loop(0, NZ, row_side, 0)
    pack_share.wait_recv()
    for k in range(NCORE):
        for dy in range(NY):
            for dx in range(NX):
                pack = col_packs[k, dy, dx]
                high, mid, low = three_parts(pack)
                feats = jnp.concatenate([high, mid, high, low, high, mid], axis=0)
                at = ((k * NY + dy) * NX + dx) * PTS
                col_feats[0:FEATS, at : at + PTS] = feats.astype(jnp.bfloat16)
                col_level[0:1, at : at + PTS] = pack[6:7, :]
    col_feats[FEATS:, :] = jnp.zeros((128 - FEATS, COLS), jnp.bfloat16)

    def kernel_rows(start, stop):
        def body(i, carry):
            at = pl.multiple_of(i * 512, 512)
            feats = col_feats[:, pl.ds(at, 512)]
            level = col_level[0:1, pl.ds(at, 512)]
            for m in range(start, stop, PTS):
                distance = jnp.dot(
                    row_feats[m : m + PTS, :], feats, preferred_element_type=jnp.float32
                )
                distance = jnp.maximum(distance, 1e-30)
                root = distance * lax.rsqrt(distance)
                levels = jnp.concatenate([row_level[m : m + PTS, :]] * 4, axis=1) + level
                tile[m : m + PTS, pl.ds(at, 512)] = jnp.exp2(levels - root).astype(jnp.bfloat16)
            return carry

        lax.fori_loop(0, COLS // 512, body, 0)

    kernel_rows(0, 3 * PTS)
    kernel_rows(3 * PTS, ROWS)
    own = slice(SLOT[0] * PTS, SLOT[0] * PTS + PTS)
    on_diagonal = lax.broadcasted_iota(jnp.int32, (PTS, PTS), 0) == lax.broadcasted_iota(
        jnp.int32, (PTS, PTS), 1
    )
    diagonal = weight * amp * amp + 1.0
    tile[own, 0:PTS] = jnp.where(
        on_diagonal, jnp.broadcast_to(diagonal, (PTS, PTS)), tile[own, 0:PTS].astype(jnp.float32)
    ).astype(jnp.bfloat16)

    up, down = {}, {}

    def share(h):
        copies = []
        for t in (2 * h, 2 * h + 1):
            for copy in second[t]:
                copy.wait_recv()
            copies.append(send(stripe.at[t, 0], stripe.at[t, 1], stripe_sems, t * 8, other))
        return copies

    def product(h, start, stop):
        right = jnp.concatenate(
            [stripe[2 * h].reshape(COLS, 128), stripe[2 * h + 1].reshape(COLS, 128)], axis=1
        )
        value = jnp.dot(
            tile[start * PTS : stop * PTS, :], right, preferred_element_type=jnp.float32
        )
        partial[h, start:stop] = value.reshape(stop - start, PTS, WIDTH)

    def half_of(h, off, half):
        return partial.at[h, SLOT[off], half * 64 : half * 64 + 64]

    def pass_on(h, i):
        for sends, plan, arrived, dz, base in (
            (up, UP, up_in, 1, 0),
            (down, DOWN, down_in, -1, 7),
        ):
            off, half = plan[i]
            mine = half_of(h, off, half)
            if i >= 2:
                sends[h, i - 2].wait_recv()
                mine[...] += arrived[h, i - 2]
            sends[h, i] = send(mine, arrived.at[h, i], ring_sems, h * 14 + base + i, device(dz=dz))

    def begin(h):
        for copy in share(h):
            copy.wait_recv()
        product(h, 0, 3)
        pass_on(h, 0)
        pass_on(h, 1)
        product(h, 3, 8)

    basis_copies = []

    def finish(h):
        for i, (a, b) in ((5, (1, 0)), (6, (0, 1))):
            up[h, i].wait_recv()
            half_of(h, 0, a)[...] += up_in[h, i]
            down[h, i].wait_recv()
            half_of(h, 0, b)[...] += down_in[h, i]
        where = slice(h * WIDTH, (h + 1) * WIDTH)
        basis[0, :, where] = partial[h, SLOT[0]]
        basis_copies.append(
            send(basis.at[0, :, where], basis.at[1, :, where], basis_sems, h, other)
        )

    begin(0)
    pass_on(0, 2)
    pass_on(0, 3)
    begin(1)
    pass_on(0, 4)
    pass_on(0, 5)
    pass_on(1, 2)
    pass_on(1, 3)
    pass_on(0, 6)
    pass_on(1, 4)
    pass_on(1, 5)
    finish(0)
    pass_on(1, 6)
    finish(1)
    for copy in basis_copies:
        copy.wait_recv()

    def columns(i):
        at = pl.multiple_of(i * 128, 128)
        return jnp.concatenate([basis[0, :, pl.ds(at, 128)], basis[1, :, pl.ds(at, 128)]], axis=0)

    for b, ((i0, j0), (i1, j1)) in enumerate(zip(*BLOCKS)):
        gram_part[:, b * 128 : (b + 1) * 128] = lax.dot_general(
            columns(i0 + core * (i1 - i0)),
            columns(j0 + core * (j1 - j0)),
            (((0,), (0,)), ((), ())),
            precision=lax.Precision.HIGH,
            preferred_element_type=jnp.float32,
        )

    def slice_at(r):
        return pl.ds(pl.multiple_of(r * 8, 8), 8)

    copies = []
    for dy, dx in PLANE:
        to = device(dy=dy, dx=dx)
        at = (-dy % NY) * NX + (-dx % NX)
        copies.append(
            send(gram_part.at[slice_at(to[0])], plane_in.at[at], gram_sems, at, to)
        )
    total = gram_part[slice_at(row), :]
    for i, copy in enumerate(copies):
        copy.wait_recv()
    for at in range(1, 16):
        total += plane_in[at]
    plane_sum[...] = total
    copies = []
    for dz in range(1, NZ):
        copies.append(
            send(plane_sum, line_in.at[NZ - dz], gram_sems, 16 + NZ - dz, device(dz=dz))
        )
    for copy in copies:
        copy.wait_recv()
    for at in range(1, NZ):
        total += line_in[at]
    line_sum[...] = total
    gram_half[core, slice_at(row), :] = total
    copies = []
    for dy, dx in PLANE:
        at = (-dy % NY) * NX + (-dx % NX)
        copies.append(
            send(
                line_sum,
                gram_half.at[core, slice_at(row)],
                gram_sems,
                24 + at,
                device(dy=dy, dx=dx),
            )
        )
    for copy in copies:
        copy.wait_recv()
    copy = send(gram_half.at[core], gram_half.at[core], gram_sems, 0, other)
    copy.wait_recv()

    norm_square = jnp.zeros((8, 128), jnp.float32)
    for k in range(NCORE):
        for b, (i, j) in enumerate(BLOCKS[k]):
            block = gram_half[k, :, b * 128 : (b + 1) * 128]
            gram[i * 128 : i * 128 + 128, j * 128 : j * 128 + 128] = block
            if i != j:
                gram[j * 128 : j * 128 + 128, i * 128 : i * 128 + 128] = block.T
            squares = jnp.sum((block * block).reshape(16, 8, 128), axis=0)
            norm_square += squares if i == j else 2.0 * squares
    scale = jnp.sqrt(jnp.sum(jnp.sum(norm_square, axis=0, keepdims=True), axis=1, keepdims=True))

    def dot(a, b):
        return jnp.dot(
            a, b, precision=lax.Precision.HIGH, preferred_element_type=jnp.float32
        )

    gram[...] = gram[...] * (1.0 / scale)
    square[...] = dot(gram[...], gram[...])
    inner = 0.0625 * square[...] - 0.5625 * gram[...]
    unit = (
        lax.broadcasted_iota(jnp.int32, (RANK, RANK), 0)
        == lax.broadcasted_iota(jnp.int32, (RANK, RANK), 1)
    ).astype(jnp.float32)
    polynomial[...] = (
        dot(square[...], inner + 1.6875 * unit) - 2.4375 * gram[...] + 2.25 * unit
    )
    start = dot(basis[0], polynomial[...])
    step = dot(start, gram[...])
    step = dot(step, polynomial[...])
    step = dot(step, polynomial[...])
    out[...] = (1.5 * start - 0.5 * step) * (math.sqrt(RANK) * lax.rsqrt(scale))

    for copy in started:
        copy.wait_send()


def per_device(points, amplitude, sketch):
    f32, bf16 = jnp.float32, jnp.bfloat16
    vmem = pl.BlockSpec(memory_space=pltpu.VMEM)
    return pl.pallas_call(
        kernel,
        out_shape=jax.ShapeDtypeStruct((PTS, RANK), f32),
        in_specs=[vmem] * 3,
        out_specs=vmem,
        scratch_shapes=[
            pltpu.VMEM((8, PTS), f32),
            pltpu.VMEM((8, PTS), f32),
            pltpu.VMEM((NZ, 8, PTS), f32),
            pltpu.VMEM((NCORE, NY, NX, 8, PTS), f32),
            pltpu.VMEM((ROWS, 128), bf16),
            pltpu.VMEM((ROWS, 128), f32),
            pltpu.VMEM((128, COLS), bf16),
            pltpu.VMEM((8, COLS), f32),
            pltpu.VMEM((ROWS, COLS), bf16),
            pltpu.VMEM((4, NCORE, NY, NX, PTS, 128), bf16),
            pltpu.VMEM((PARTS, NZ, PTS, WIDTH), f32),
            pltpu.VMEM((PARTS, 7, 64, WIDTH), f32),
            pltpu.VMEM((PARTS, 7, 64, WIDTH), f32),
            pltpu.VMEM((NCORE, PTS, RANK), f32),
            pltpu.VMEM((128, 640), f32),
            pltpu.VMEM((16, 8, 640), f32),
            pltpu.VMEM((8, 640), f32),
            pltpu.VMEM((NZ, 8, 640), f32),
            pltpu.VMEM((8, 640), f32),
            pltpu.VMEM((NCORE, 128, 640), f32),
            pltpu.VMEM((RANK, RANK), f32),
            pltpu.VMEM((RANK, RANK), f32),
            pltpu.VMEM((RANK, RANK), f32),
            pltpu.SemaphoreType.DMA((2, 24)),
            pltpu.SemaphoreType.DMA((2, 32)),
            pltpu.SemaphoreType.DMA((2, 14 * PARTS)),
            pltpu.SemaphoreType.DMA((2, PARTS)),
            pltpu.SemaphoreType.DMA((2, 40)),
        ],
        compiler_params=pltpu.CompilerParams(
            collective_id=0, has_side_effects=True, vmem_limit_bytes=56 << 20
        ),
        cost_estimate=pl.CostEstimate(
            flops=7_000_000_000, bytes_accessed=1 << 20, transcendentals=8 << 20
        ),
        name="kl_modes",
    )(points, amplitude.reshape(1, -1), sketch)


def solution(mesh):
    in_specs = (P(None, ("row", "col")), P(("row", "col")), P(("row", "col"), None))
    out_specs = P(("row", "col"), None)
    return jax.shard_map(
        per_device, mesh=mesh, in_specs=in_specs, out_specs=out_specs, check_vma=False
    )
```

```python
import math

import jax
import jax.numpy as jnp
from jax import lax
from jax.experimental import pallas as pl
from jax.experimental.pallas import tpu as pltpu
from jax.sharding import PartitionSpec as P

NS_ITERS = 3
CORRELATION = 4.0

MESH = pl.DeviceIdType.MESH
NX, NY, NZ, NCORE = 4, 4, 8, 2
PTS = 128
RANK = 512
WIDTH = 128
PARTS = RANK // WIDTH
HALF = PTS // 2
ROWS = NZ * PTS
COLS = NX * NY * NCORE * PTS
FEATS = 48
OFFSETS = (4, 3, -3, 2, -2, 1, -1, 0)
SLOT = {off: i for i, off in enumerate(OFFSETS)}
UP = ((4, 0), (3, 1), (3, 0), (2, 1), (2, 0), (1, 1), (1, 0))
DOWN = ((4, 1), (-3, 0), (-3, 1), (-2, 0), (-2, 1), (-1, 0), (-1, 1))
BLOCKS = (
    ((0, 0), (0, 1), (1, 1), (0, 3), (1, 3)),
    ((0, 2), (1, 2), (2, 2), (2, 3), (3, 3)),
)
GROUPS = ((0, 3), (3, 5))
ORDER = (
    ("share", 0), ("kernel", 0, 1), ("kernel", 1, 3), ("share", 1), ("first", 0), ("second", 0),
    ("kernel", 3, 5), ("share", 2), ("first", 1), ("second", 1), ("pass", 0, 2), ("share", 3),
    ("first", 2), ("second", 2), ("third", 0), ("pass", 0, 3), ("first", 3), ("pass", 1, 2),
    ("second", 3), ("third", 1), ("pass", 0, 4), ("pass", 1, 3), ("third", 2), ("pass", 2, 2),
    ("pass", 2, 3), ("third", 3), ("kernel", 5, 7), ("pass", 1, 4), ("pass", 3, 2), ("kernel", 7, 8),
    ("pass", 3, 3), ("fourth", 0), ("pass", 0, 5), ("pass", 0, 6), ("last", 0), ("pass", 2, 4),
    ("fourth", 1), ("pass", 1, 5), ("last", 1), ("fourth", 2), ("pass", 1, 6), ("pass", 2, 5),
    ("pass", 3, 4), ("last", 2), ("fourth", 3), ("pass", 3, 5), ("last", 3), ("finish", 0),
    ("pass", 2, 6), ("finish", 1), ("pass", 3, 6), ("finish", 2),
)
PLANE = tuple((dy, dx) for dy in range(NY) for dx in range(NX) if (dy, dx) != (0, 0))


def three_parts(v):
    high = v.astype(jnp.bfloat16).astype(jnp.float32)
    rest = v - high
    mid = rest.astype(jnp.bfloat16).astype(jnp.float32)
    low = (rest - mid).astype(jnp.bfloat16).astype(jnp.float32)
    return high, mid, low


def kernel(
    points,
    amplitude,
    sketch,
    out,
    row_pack,
    col_pack,
    row_packs,
    col_packs,
    row_feats,
    row_level,
    col_feats,
    col_level,
    tile,
    stripe,
    partial,
    up_in,
    down_in,
    basis,
    gram_part,
    plane_in,
    plane_sum,
    line_in,
    line_sum,
    gram_half,
    gram,
    square,
    polynomial,
    pack_sems,
    stripe_sems,
    ring_sems,
    basis_sems,
    gram_sems,
    ready,
):
    row = lax.axis_index("row")
    col = lax.axis_index("col")
    y, x = lax.div(row, NX), lax.rem(row, NX)
    z, core = lax.div(col, NCORE), lax.rem(col, NCORE)

    def device(dy=0, dx=0, dz=0, dcore=0):
        return (
            lax.rem(y + dy + NY, NY) * NX + lax.rem(x + dx + NX, NX),
            lax.rem(z + dz + NZ, NZ) * NCORE + lax.rem(core + dcore + NCORE, NCORE),
        )

    def send(src, dst, sems, index, to):
        copy = pltpu.make_async_remote_copy(
            src_ref=src,
            dst_ref=dst,
            send_sem=sems.at[0, index],
            recv_sem=sems.at[1, index],
            device_id=to,
            device_id_type=MESH,
        )
        copy.start()
        started.append(copy)
        return copy

    started = []
    other = device(dcore=1)

    barrier = pltpu.get_barrier_semaphore()

    def report(to_core, **where):
        pl.semaphore_signal(
            barrier, inc=1, device_id=device(dcore=to_core - core, **where), device_id_type=MESH
        )

    for d in range(1, 4):
        report(0, dx=d)
        report(0, dy=d)
    pl.semaphore_signal(barrier, inc=1, device_id=other, device_id_type=MESH)
    for dz in range(1, NZ):
        report(1, dz=dz)

    weight = 0.5 / math.sqrt(ROWS * NX * NY * NCORE)
    per_unit = 1.0 / (CORRELATION * math.log(2.0))
    amp = amplitude[...]
    level = jnp.log(amp) * (1.0 / math.log(2.0)) + 0.5 * math.log2(weight)
    ux = (points[0:1, :] - 0.5) * per_unit
    uy = (points[1:2, :] - 0.5) * per_unit
    uz = (points[2:3, :] - 4.0) * per_unit
    norm = ux * ux + uy * uy + uz * uz
    row_pack[...] = jnp.zeros_like(row_pack)
    col_pack[...] = jnp.zeros_like(col_pack)
    for i, v in enumerate((ux, uy, uz)):
        row_pack[i : i + 1, :] = v
        col_pack[i : i + 1, :] = -2.0 * v
    row_pack[3:4, :] = norm
    row_pack[4:5, :] = jnp.ones_like(norm)
    row_pack[5:6, :] = level
    col_pack[3:4, :] = jnp.ones_like(norm)
    col_pack[4:5, :] = norm
    col_pack[6:7, :] = level
    row_packs[SLOT[0]] = row_pack[...]
    col_packs[0, 0, 0] = col_pack[...]
    for t in range(4):
        stripe[t, 0, 0, 0] = sketch[:, t * 128 : (t + 1) * 128]

    @pl.when(core == 0)
    def _():
        pl.semaphore_wait(barrier, 13)
        pl.semaphore_signal(ready, inc=1, device_id=other, device_id_type=MESH)

    @pl.when(core == 1)
    def _():
        pl.semaphore_wait(ready, 1)

    near, far = slice(0, HALF), slice(HALF, PTS)

    def first_stage(t):
        copies = []
        where = slice(t * WIDTH, (t + 1) * WIDTH)
        for d in range(1, 4):
            copies.append(
                send(
                    sketch.at[near, where],
                    stripe.at[t, 0, 0, -d % NX, near],
                    stripe_sems,
                    t * 16 + d,
                    device(dx=d),
                )
            )
            copies.append(
                send(
                    sketch.at[far, where],
                    stripe.at[t, 0, -d % NY, 0, far],
                    stripe_sems,
                    t * 16 + 3 + d,
                    device(dy=d),
                )
            )
        return copies

    def second_stage(t):
        for copy in first[t]:
            copy.wait_recv()
        copies = []
        for d in range(1, 4):
            copies.append(
                send(
                    stripe.at[t, 0, 0, :, near],
                    stripe.at[t, 0, -d % NY, :, near],
                    stripe_sems,
                    t * 16 + 6 + d,
                    device(dy=d),
                )
            )
            copies.append(
                send(
                    stripe.at[t, 0, :, 0, far],
                    stripe.at[t, 0, :, -d % NX, far],
                    stripe_sems,
                    t * 16 + 9 + d,
                    device(dx=d),
                )
            )
        return copies

    packs_x = [
        send(col_pack, col_packs.at[0, 0, -d % NX], pack_sems, 8 + d, device(dx=d))
        for d in range(1, 4)
    ]
    first = {t: first_stage(t) for t in range(PARTS)}

    @pl.when(core == 1)
    def _():
        pl.semaphore_wait(barrier, 15)
        pl.semaphore_signal(ready, inc=1, device_id=other, device_id_type=MESH)

    @pl.when(core == 0)
    def _():
        pl.semaphore_wait(ready, 1)

    line_packs = []
    for dz in range(1, NZ):
        at = SLOT[-dz if dz <= 3 else 8 - dz]
        line_packs.append(send(row_pack, row_packs.at[at], pack_sems, at, device(dz=dz)))
    for copy in packs_x:
        copy.wait_recv()
    packs_y = [
        send(col_packs.at[0, 0], col_packs.at[0, -d % NY], pack_sems, 11 + d, device(dy=d))
        for d in range(1, 4)
    ]
    second = {t: second_stage(t) for t in range(PARTS)}
    for copy in packs_y:
        copy.wait_recv()
    pack_share = send(col_packs.at[0], col_packs.at[1], pack_sems, 8, other)

    def row_side(i, carry):
        pack = row_packs[i]
        high, mid, low = three_parts(pack)
        feats = jnp.concatenate([high, high, mid, high, low, mid], axis=0)
        feats = jnp.concatenate([feats, jnp.zeros((128 - FEATS, PTS), jnp.float32)], axis=0)
        at = pl.multiple_of(i * PTS, PTS)
        row_feats[pl.ds(at, PTS), :] = feats.T.astype(jnp.bfloat16)
        row_level[pl.ds(at, PTS), :] = jnp.broadcast_to(pack[5:6, :], (PTS, PTS)).T
        return carry

    def column_side(k):
        for dy in range(NY):
            for dx in range(NX):
                pack = col_packs[k, dy, dx]
                high, mid, low = three_parts(pack)
                feats = jnp.concatenate([high, mid, high, low, high, mid], axis=0)
                at = ((k * NY + dy) * NX + dx) * PTS
                col_feats[0:FEATS, at : at + PTS] = feats.astype(jnp.bfloat16)
                col_level[0:1, at : at + PTS] = pack[6:7, :]

    col_feats[FEATS:, :] = jnp.zeros((128 - FEATS, COLS), jnp.bfloat16)
    column_side(0)
    pack_share.wait_recv()
    column_side(1)
    for copy in line_packs:
        copy.wait_recv()
    lax.fori_loop(0, NZ, row_side, 0)

    def kernel_rows(start, stop):
        def body(i, carry):
            at = pl.multiple_of(i * 512, 512)
            feats = col_feats[:, pl.ds(at, 512)]
            level = col_level[0:1, pl.ds(at, 512)]
            for m in range(start, stop, PTS):
                distance = jnp.dot(
                    row_feats[m : m + PTS, :], feats, preferred_element_type=jnp.float32
                )
                distance = jnp.maximum(distance, 1e-30)
                root = distance * lax.rsqrt(distance)
                levels = jnp.concatenate([row_level[m : m + PTS, :]] * 4, axis=1) + level
                tile[m : m + PTS, pl.ds(at, 512)] = jnp.exp2(levels - root).astype(jnp.bfloat16)
            return carry

        lax.fori_loop(0, COLS // 512, body, 0)

    def place_diagonal():
        own = slice(SLOT[0] * PTS, SLOT[0] * PTS + PTS)
        on_diagonal = lax.broadcasted_iota(jnp.int32, (PTS, PTS), 0) == lax.broadcasted_iota(
            jnp.int32, (PTS, PTS), 1
        )
        diagonal = jnp.broadcast_to(weight * amp * amp + 1.0, (PTS, PTS))
        tile[own, 0:PTS] = jnp.where(
            on_diagonal, diagonal, tile[own, 0:PTS].astype(jnp.float32)
        ).astype(jnp.bfloat16)

    up, down, shares = {}, {}, {}

    def share(c):
        for copy in second[c]:
            copy.wait_recv()
        shares[c] = send(stripe.at[c, 0], stripe.at[c, 1], stripe_sems, c * 16, other)

    def block_product(c, start, stop):
        partial[c, start:stop] = jnp.dot(
            tile[start * PTS : stop * PTS, :],
            stripe[c].reshape(COLS, WIDTH),
            preferred_element_type=jnp.float32,
        ).reshape(stop - start, PTS, WIDTH)

    def half_of(c, off, half):
        return partial.at[c, SLOT[off], half * HALF : (half + 1) * HALF]

    def pass_on(c, *steps):
        for i in steps:
            for sends, plan, arrived, dz, base in (
                (up, UP, up_in, 1, 0),
                (down, DOWN, down_in, -1, 7),
            ):
                off, half = plan[i]
                mine = half_of(c, off, half)
                if i >= 2:
                    sends[c, i - 2].wait_recv()
                    mine[...] += arrived[c, i - 2]
                sends[c, i] = send(
                    mine, arrived.at[c, i], ring_sems, c * 14 + base + i, device(dz=dz)
                )

    def first_product(c):
        shares[c].wait_recv()
        block_product(c, 0, 1)
        pass_on(c, 0)

    def second_product(c):
        block_product(c, 1, 3)
        pass_on(c, 1)

    def kernel_blocks(start, stop):
        kernel_rows(start * PTS, stop * PTS)
        if stop == NZ:
            place_diagonal()

    basis_copies = []

    def finish(c):
        for i, (a, b) in ((5, (1, 0)), (6, (0, 1))):
            up[c, i].wait_recv()
            half_of(c, 0, a)[...] += up_in[c, i]
            down[c, i].wait_recv()
            half_of(c, 0, b)[...] += down_in[c, i]
        where = slice(c * WIDTH, (c + 1) * WIDTH)
        basis[0, :, where] = partial[c, SLOT[0]]
        basis_copies.append(
            send(basis.at[0, :, where], basis.at[1, :, where], basis_sems, c, other)
        )

    def columns(i):
        at = pl.multiple_of(i * 128, 128)
        return jnp.concatenate([basis[0, :, pl.ds(at, 128)], basis[1, :, pl.ds(at, 128)]], axis=0)

    def slice_at(r):
        return pl.ds(pl.multiple_of(r * 8, 8), 8)

    def lanes(g):
        return slice(GROUPS[g][0] * 128, GROUPS[g][1] * 128)

    def chip_blocks(g):
        for b in range(*GROUPS[g]):
            (i0, j0), (i1, j1) = BLOCKS[0][b], BLOCKS[1][b]
            gram_part[:, b * 128 : (b + 1) * 128] = lax.dot_general(
                columns(i0 + core * (i1 - i0)),
                columns(j0 + core * (j1 - j0)),
                (((0,), (0,)), ((), ())),
                precision=lax.Precision.HIGH,
                preferred_element_type=jnp.float32,
            )
        copies = []
        for dy, dx in PLANE:
            to = device(dy=dy, dx=dx)
            at = (-dy % NY) * NX + (-dx % NX)
            copies.append(
                send(
                    gram_part.at[slice_at(to[0]), lanes(g)],
                    plane_in.at[at, :, lanes(g)],
                    gram_sems,
                    g * 40 + at,
                    to,
                )
            )
        return copies

    def over_plane(g, copies):
        for copy in copies:
            copy.wait_recv()
        total = gram_part[slice_at(row), lanes(g)]
        for at in range(1, 16):
            total += plane_in[at, :, lanes(g)]
        plane_sum[:, lanes(g)] = total
        return [
            send(
                plane_sum.at[:, lanes(g)],
                line_in.at[NZ - dz, :, lanes(g)],
                gram_sems,
                g * 40 + 16 + NZ - dz,
                device(dz=dz),
            )
            for dz in range(1, NZ)
        ]

    def over_line(g, copies):
        for copy in copies:
            copy.wait_recv()
        total = plane_sum[:, lanes(g)]
        for at in range(1, NZ):
            total += line_in[at, :, lanes(g)]
        line_sum[:, lanes(g)] = total
        gram_half[core, slice_at(row), lanes(g)] = total
        return [
            send(
                line_sum.at[:, lanes(g)],
                gram_half.at[core, slice_at(row), lanes(g)],
                gram_sems,
                g * 40 + 24 + (-dy % NY) * NX + (-dx % NX),
                device(dy=dy, dx=dx),
            )
            for dy, dx in PLANE
        ]

    def to_other(g, copies):
        for copy in copies:
            copy.wait_recv()
        half = gram_half.at[core, :, lanes(g)]
        return send(half, half, gram_sems, g * 40, other)

    work = {
        "share": share,
        "kernel": kernel_blocks,
        "first": first_product,
        "second": second_product,
        "third": lambda c: block_product(c, 3, 5),
        "fourth": lambda c: block_product(c, 5, 7),
        "last": lambda c: block_product(c, 7, 8),
        "pass": pass_on,
        "finish": finish,
    }
    for name, *which in ORDER:
        work[name](*which)
    for copy in basis_copies:
        copy.wait_recv()
    early = chip_blocks(0)
    finish(3)
    basis_copies[3].wait_recv()
    late = chip_blocks(1)
    early = over_plane(0, early)
    late = over_plane(1, late)
    early = over_line(0, early)
    late = over_line(1, late)
    early = to_other(0, early)
    late = to_other(1, late)
    early.wait_recv()
    late.wait_recv()

    norm_square = jnp.zeros((8, 128), jnp.float32)
    for k in range(NCORE):
        for b, (i, j) in enumerate(BLOCKS[k]):
            block = gram_half[k, :, b * 128 : (b + 1) * 128]
            gram[i * 128 : i * 128 + 128, j * 128 : j * 128 + 128] = block
            if i != j:
                gram[j * 128 : j * 128 + 128, i * 128 : i * 128 + 128] = block.T
            squares = jnp.sum((block * block).reshape(16, 8, 128), axis=0)
            norm_square += squares if i == j else 2.0 * squares
    scale = jnp.sqrt(jnp.sum(jnp.sum(norm_square, axis=0, keepdims=True), axis=1, keepdims=True))

    def dot(a, b):
        return jnp.dot(
            a, b, precision=lax.Precision.HIGH, preferred_element_type=jnp.float32
        )

    gram[...] = gram[...] * (1.0 / scale)
    square[...] = dot(gram[...], gram[...])
    inner = 0.0625 * square[...] - 0.5625 * gram[...]
    unit = (
        lax.broadcasted_iota(jnp.int32, (RANK, RANK), 0)
        == lax.broadcasted_iota(jnp.int32, (RANK, RANK), 1)
    ).astype(jnp.float32)
    polynomial[...] = (
        dot(square[...], inner + 1.6875 * unit) - 2.4375 * gram[...] + 2.25 * unit
    )
    start = dot(basis[0], polynomial[...])
    step = dot(start, gram[...])
    step = dot(step, polynomial[...])
    step = dot(step, polynomial[...])
    out[...] = (1.5 * start - 0.5 * step) * (math.sqrt(RANK) * lax.rsqrt(scale))

    for copy in started:
        copy.wait_send()


def per_device(points, amplitude, sketch):
    f32, bf16 = jnp.float32, jnp.bfloat16
    vmem = pl.BlockSpec(memory_space=pltpu.VMEM)
    return pl.pallas_call(
        kernel,
        out_shape=jax.ShapeDtypeStruct((PTS, RANK), f32),
        in_specs=[vmem] * 3,
        out_specs=vmem,
        scratch_shapes=[
            pltpu.VMEM((8, PTS), f32),
            pltpu.VMEM((8, PTS), f32),
            pltpu.VMEM((NZ, 8, PTS), f32),
            pltpu.VMEM((NCORE, NY, NX, 8, PTS), f32),
            pltpu.VMEM((ROWS, 128), bf16),
            pltpu.VMEM((ROWS, 128), f32),
            pltpu.VMEM((128, COLS), bf16),
            pltpu.VMEM((8, COLS), f32),
            pltpu.VMEM((ROWS, COLS), bf16),
            pltpu.VMEM((PARTS, NCORE, NY, NX, PTS, WIDTH), bf16),
            pltpu.VMEM((PARTS, NZ, PTS, WIDTH), f32),
            pltpu.VMEM((PARTS, 7, HALF, WIDTH), f32),
            pltpu.VMEM((PARTS, 7, HALF, WIDTH), f32),
            pltpu.VMEM((NCORE, PTS, RANK), f32),
            pltpu.VMEM((128, 640), f32),
            pltpu.VMEM((16, 8, 640), f32),
            pltpu.VMEM((8, 640), f32),
            pltpu.VMEM((NZ, 8, 640), f32),
            pltpu.VMEM((8, 640), f32),
            pltpu.VMEM((NCORE, 128, 640), f32),
            pltpu.VMEM((RANK, RANK), f32),
            pltpu.VMEM((RANK, RANK), f32),
            pltpu.VMEM((RANK, RANK), f32),
            pltpu.SemaphoreType.DMA((2, 24)),
            pltpu.SemaphoreType.DMA((2, 16 * PARTS)),
            pltpu.SemaphoreType.DMA((2, 14 * PARTS)),
            pltpu.SemaphoreType.DMA((2, PARTS)),
            pltpu.SemaphoreType.DMA((2, 80)),
            pltpu.SemaphoreType.REGULAR,
        ],
        compiler_params=pltpu.CompilerParams(
            collective_id=0, has_side_effects=True, vmem_limit_bytes=56 << 20
        ),
        cost_estimate=pl.CostEstimate(
            flops=7_000_000_000, bytes_accessed=1 << 20, transcendentals=8 << 20
        ),
        name="kl_modes",
    )(points, amplitude.reshape(1, -1), sketch)


def solution(mesh):
    in_specs = (P(None, ("row", "col")), P(("row", "col")), P(("row", "col"), None))
    out_specs = P(("row", "col"), None)
    return jax.shard_map(
        per_device, mesh=mesh, in_specs=in_specs, out_specs=out_specs, check_vma=False
    )
```

```python
import math

import jax
import jax.numpy as jnp
from jax import lax
from jax.experimental import pallas as pl
from jax.experimental.pallas import tpu as pltpu
from jax.sharding import PartitionSpec as P

NS_ITERS = 3
CORRELATION = 4.0

MESH = pl.DeviceIdType.MESH
NX, NY, NZ, NCORE = 4, 4, 8, 2
PTS = 128
RANK = 512
WIDTH = 128
PARTS = RANK // WIDTH
HALF = PTS // 2
LANES = 1024
ROWS = NZ * PTS
COLS = NX * NY * NCORE * PTS
FEATS = 48
OFFSETS = (4, 3, -3, 2, -2, 1, -1, 0)
SLOT = {off: i for i, off in enumerate(OFFSETS)}
UP = ((4, 0), (3, 1), (3, 0), (2, 1), (2, 0), (1, 1), (1, 0))
DOWN = ((4, 1), (-3, 0), (-3, 1), (-2, 0), (-2, 1), (-1, 0), (-1, 1))
BLOCKS = (
    ((0, 0), (0, 1), (1, 1), (0, 3), (1, 3)),
    ((0, 2), (1, 2), (2, 2), (2, 3), (3, 3)),
)
GROUPS = ((0, 3), (3, 5))
ORDER = (
    ("kernel", 0, 1), ("share", 0), ("share", 1), ("kernel", 1, 3), ("first", 0), ("first", 1),
    ("share", 2), ("second", 0), ("second", 1), ("first", 2), ("second", 2), ("kernel", 3, 5),
    ("pass", 1, 2), ("share", 3), ("pass", 0, 2), ("third", 0), ("pass", 0, 3), ("pass", 1, 3),
    ("first", 3), ("pass", 2, 2), ("second", 3), ("kernel", 5, 7), ("pass", 0, 4), ("pass", 1, 4),
    ("fourth", 0), ("pass", 1, 5), ("pass", 0, 5), ("pass", 3, 2), ("third", 1), ("pass", 2, 3),
    ("pass", 2, 4), ("pass", 3, 3), ("fourth", 1), ("pass", 0, 6), ("last", 1), ("pass", 1, 6),
    ("last", 0), ("pass", 3, 4), ("pass", 2, 5), ("pass", 2, 6), ("pass", 3, 5), ("finish", 0),
    ("finish", 1), ("pass", 3, 6), ("finish", 2),
)
PLANE = tuple(
    sorted(
        ((dy, dx) for dy in range(NY) for dx in range(NX) if (dy, dx) != (0, 0)),
        key=lambda p: -(min(p[0], NY - p[0]) + min(p[1], NX - p[1])),
    )
)
LINE = tuple(sorted(range(1, NZ), key=lambda d: -min(d, NZ - d)))


def three_parts(v):
    high = v.astype(jnp.bfloat16).astype(jnp.float32)
    rest = v - high
    mid = rest.astype(jnp.bfloat16).astype(jnp.float32)
    low = (rest - mid).astype(jnp.bfloat16).astype(jnp.float32)
    return high, mid, low


def kernel(
    points,
    amplitude,
    sketch,
    out,
    row_pack,
    col_pack,
    row_packs,
    col_packs,
    row_feats,
    row_level,
    col_feats,
    col_level,
    tile,
    stripe,
    partial,
    up_in,
    down_in,
    basis,
    gram_part,
    plane_in,
    plane_sum,
    line_in,
    line_sum,
    gram_half,
    gram,
    square,
    polynomial,
    pack_sems,
    stripe_sems,
    ring_sems,
    basis_sems,
    gram_sems,
    ready,
):
    row = lax.axis_index("row")
    col = lax.axis_index("col")
    y, x = lax.div(row, NX), lax.rem(row, NX)
    z, core = lax.div(col, NCORE), lax.rem(col, NCORE)

    def device(dy=0, dx=0, dz=0, dcore=0):
        return (
            lax.rem(y + dy + NY, NY) * NX + lax.rem(x + dx + NX, NX),
            lax.rem(z + dz + NZ, NZ) * NCORE + lax.rem(core + dcore + NCORE, NCORE),
        )

    def send(src, dst, sems, index, to):
        copy = pltpu.make_async_remote_copy(
            src_ref=src,
            dst_ref=dst,
            send_sem=sems.at[0, index],
            recv_sem=sems.at[1, index],
            device_id=to,
            device_id_type=MESH,
        )
        copy.start()
        started.append(copy)
        return copy

    started = []
    other = device(dcore=1)

    barrier = pltpu.get_barrier_semaphore()

    def report(to_core, **where):
        pl.semaphore_signal(
            barrier, inc=1, device_id=device(dcore=to_core - core, **where), device_id_type=MESH
        )

    for dz in LINE:
        report(1, dz=dz)
    for d in range(1, 4):
        report(0, dx=d)
        report(0, dy=d)
    pl.semaphore_signal(barrier, inc=1, device_id=other, device_id_type=MESH)

    weight = 0.5 / math.sqrt(ROWS * NX * NY * NCORE)
    per_unit = 1.0 / (CORRELATION * math.log(2.0))
    amp = amplitude[...]
    level = jnp.log(amp) * (1.0 / math.log(2.0)) + 0.5 * math.log2(weight)
    ux = (points[0:1, :] - 0.5) * per_unit
    uy = (points[1:2, :] - 0.5) * per_unit
    uz = (points[2:3, :] - 4.0) * per_unit
    norm = ux * ux + uy * uy + uz * uz
    row_pack[...] = jnp.zeros_like(row_pack)
    col_pack[...] = jnp.zeros_like(col_pack)
    for i, v in enumerate((ux, uy, uz)):
        row_pack[i : i + 1, :] = v
        col_pack[i : i + 1, :] = -2.0 * v
    row_pack[3:4, :] = norm
    row_pack[4:5, :] = jnp.ones_like(norm)
    row_pack[5:6, :] = level
    col_pack[3:4, :] = jnp.ones_like(norm)
    col_pack[4:5, :] = norm
    col_pack[6:7, :] = level
    row_packs[SLOT[0]] = row_pack[...]
    col_packs[0, 0, 0] = col_pack[...]
    for t in range(4):
        stripe[t, 0, 0, 0] = sketch[:, t * 128 : (t + 1) * 128]

    @pl.when(core == 0)
    def _():
        pl.semaphore_wait(barrier, 13)
        pl.semaphore_signal(ready, inc=1, device_id=other, device_id_type=MESH)

    @pl.when(core == 1)
    def _():
        pl.semaphore_wait(ready, 1)

    near, far = slice(0, HALF), slice(HALF, PTS)

    def first_stage(t):
        copies = []
        where = slice(t * WIDTH, (t + 1) * WIDTH)
        for d in range(1, 4):
            copies.append(
                send(
                    sketch.at[near, where],
                    stripe.at[t, 0, 0, -d % NX, near],
                    stripe_sems,
                    t * 16 + d,
                    device(dx=d),
                )
            )
            copies.append(
                send(
                    sketch.at[far, where],
                    stripe.at[t, 0, -d % NY, 0, far],
                    stripe_sems,
                    t * 16 + 3 + d,
                    device(dy=d),
                )
            )
        return copies

    def second_stage(t):
        for copy in first[t]:
            copy.wait_recv()
        copies = []
        for d in range(1, 4):
            copies.append(
                send(
                    stripe.at[t, 0, 0, :, near],
                    stripe.at[t, 0, -d % NY, :, near],
                    stripe_sems,
                    t * 16 + 6 + d,
                    device(dy=d),
                )
            )
            copies.append(
                send(
                    stripe.at[t, 0, :, 0, far],
                    stripe.at[t, 0, :, -d % NX, far],
                    stripe_sems,
                    t * 16 + 9 + d,
                    device(dx=d),
                )
            )
        return copies

    packs_x = [
        send(col_pack, col_packs.at[0, 0, -d % NX], pack_sems, 8 + d, device(dx=d))
        for d in range(1, 4)
    ]
    first = {t: first_stage(t) for t in range(PARTS)}

    @pl.when(core == 1)
    def _():
        pl.semaphore_wait(barrier, 15)
        pl.semaphore_signal(ready, inc=1, device_id=other, device_id_type=MESH)

    @pl.when(core == 0)
    def _():
        pl.semaphore_wait(ready, 1)

    line_packs = []
    for dz in LINE:
        at = SLOT[-dz if dz <= 3 else 8 - dz]
        line_packs.append(send(row_pack, row_packs.at[at], pack_sems, at, device(dz=dz)))
    for copy in packs_x:
        copy.wait_recv()
    packs_y = [
        send(col_packs.at[0, 0], col_packs.at[0, -d % NY], pack_sems, 11 + d, device(dy=d))
        for d in range(1, 4)
    ]
    second = {t: second_stage(t) for t in range(PARTS)}
    for copy in packs_y:
        copy.wait_recv()
    pack_share = send(col_packs.at[0], col_packs.at[1], pack_sems, 8, other)

    def row_side(i, carry):
        pack = row_packs[i]
        high, mid, low = three_parts(pack)
        feats = jnp.concatenate([high, high, mid, high, low, mid], axis=0)
        feats = jnp.concatenate([feats, jnp.zeros((128 - FEATS, PTS), jnp.float32)], axis=0)
        at = pl.multiple_of(i * PTS, PTS)
        row_feats[pl.ds(at, PTS), :] = feats.T.astype(jnp.bfloat16)
        row_level[pl.ds(at, PTS), :] = jnp.broadcast_to(pack[5:6, :], (PTS, PTS)).T
        return carry

    def column_side(k):
        for dy in range(NY):
            for dx in range(NX):
                pack = col_packs[k, dy, dx]
                high, mid, low = three_parts(pack)
                feats = jnp.concatenate([high, mid, high, low, high, mid], axis=0)
                at = ((k * NY + dy) * NX + dx) * PTS
                col_feats[0:FEATS, at : at + PTS] = feats.astype(jnp.bfloat16)
                col_level[0:1, at : at + PTS] = pack[6:7, :]

    col_feats[FEATS:, :] = jnp.zeros((128 - FEATS, COLS), jnp.bfloat16)
    column_side(0)
    pack_share.wait_recv()
    column_side(1)
    row_side(SLOT[0], 0)

    def kernel_rows(start, stop):
        def body(i, carry):
            at = pl.multiple_of(i * LANES, LANES)
            feats = col_feats[:, pl.ds(at, LANES)]
            level = col_level[0:1, pl.ds(at, LANES)]
            for m in range(start, stop, PTS):
                distance = jnp.dot(
                    row_feats[m : m + PTS, :], feats, preferred_element_type=jnp.float32
                )
                distance = jnp.maximum(distance, 1e-30)
                root = distance * lax.rsqrt(distance)
                levels = jnp.concatenate([row_level[m : m + PTS, :]] * (LANES // PTS), axis=1)
                tile[m : m + PTS, pl.ds(at, LANES)] = jnp.exp2(levels + level - root).astype(
                    jnp.bfloat16
                )
            return carry

        lax.fori_loop(0, COLS // LANES, body, 0)

    def place_diagonal():
        own = slice(SLOT[0] * PTS, SLOT[0] * PTS + PTS)
        on_diagonal = lax.broadcasted_iota(jnp.int32, (PTS, PTS), 0) == lax.broadcasted_iota(
            jnp.int32, (PTS, PTS), 1
        )
        diagonal = jnp.broadcast_to(weight * amp * amp + 1.0, (PTS, PTS))
        tile[own, 0:PTS] = jnp.where(
            on_diagonal, diagonal, tile[own, 0:PTS].astype(jnp.float32)
        ).astype(jnp.bfloat16)

    kernel_rows(SLOT[0] * PTS, NZ * PTS)
    place_diagonal()
    for copy in line_packs:
        copy.wait_recv()
    lax.fori_loop(0, SLOT[0], row_side, 0)

    up, down, shares = {}, {}, {}

    def share(c):
        for copy in second[c]:
            copy.wait_recv()
        shares[c] = send(stripe.at[c, 0], stripe.at[c, 1], stripe_sems, c * 16, other)

    def block_product(c, start, stop):
        partial[c, start:stop] = jnp.dot(
            tile[start * PTS : stop * PTS, :],
            stripe[c].reshape(COLS, WIDTH),
            preferred_element_type=jnp.float32,
        ).reshape(stop - start, PTS, WIDTH)

    def pair_product(p, start, stop):
        chunks = (2 * p, 2 * p + 1)
        value = jnp.dot(
            tile[start * PTS : stop * PTS, :],
            jnp.concatenate([stripe[c].reshape(COLS, WIDTH) for c in chunks], axis=1),
            preferred_element_type=jnp.float32,
        )
        for i, c in enumerate(chunks):
            partial[c, start:stop] = value[:, i * WIDTH : (i + 1) * WIDTH].reshape(
                stop - start, PTS, WIDTH
            )

    def half_of(c, off, half):
        return partial.at[c, SLOT[off], half * HALF : (half + 1) * HALF]

    def pass_on(c, *steps):
        for i in steps:
            for sends, plan, arrived, dz, base in (
                (up, UP, up_in, 1, 0),
                (down, DOWN, down_in, -1, 7),
            ):
                off, half = plan[i]
                mine = half_of(c, off, half)
                if i >= 2:
                    sends[c, i - 2].wait_recv()
                    mine[...] += arrived[c, i - 2]
                sends[c, i] = send(
                    mine, arrived.at[c, i], ring_sems, c * 14 + base + i, device(dz=dz)
                )

    def first_product(c):
        shares[c].wait_recv()
        block_product(c, 0, 1)
        pass_on(c, 0)

    def second_product(c):
        block_product(c, 1, 3)
        pass_on(c, 1)

    basis_copies = []

    def finish(c):
        for i, (a, b) in ((5, (1, 0)), (6, (0, 1))):
            up[c, i].wait_recv()
            half_of(c, 0, a)[...] += up_in[c, i]
            down[c, i].wait_recv()
            half_of(c, 0, b)[...] += down_in[c, i]
        where = slice(c * WIDTH, (c + 1) * WIDTH)
        basis[0, :, where] = partial[c, SLOT[0]]
        basis_copies.append(
            send(basis.at[0, :, where], basis.at[1, :, where], basis_sems, c, other)
        )

    def columns(i):
        at = pl.multiple_of(i * 128, 128)
        return jnp.concatenate([basis[0, :, pl.ds(at, 128)], basis[1, :, pl.ds(at, 128)]], axis=0)

    def slice_at(r):
        return pl.ds(pl.multiple_of(r * 8, 8), 8)

    def lanes(g):
        return slice(GROUPS[g][0] * 128, GROUPS[g][1] * 128)

    def chip_blocks(g):
        for b in range(*GROUPS[g]):
            (i0, j0), (i1, j1) = BLOCKS[0][b], BLOCKS[1][b]
            gram_part[:, b * 128 : (b + 1) * 128] = lax.dot_general(
                columns(i0 + core * (i1 - i0)),
                columns(j0 + core * (j1 - j0)),
                (((0,), (0,)), ((), ())),
                precision=lax.Precision.HIGH,
                preferred_element_type=jnp.float32,
            )
        copies = []
        for dy, dx in PLANE:
            to = device(dy=dy, dx=dx)
            at = (-dy % NY) * NX + (-dx % NX)
            copies.append(
                send(
                    gram_part.at[slice_at(to[0]), lanes(g)],
                    plane_in.at[at, :, lanes(g)],
                    gram_sems,
                    g * 40 + at,
                    to,
                )
            )
        return copies

    def over_plane(g, copies):
        for copy in copies:
            copy.wait_recv()
        total = gram_part[slice_at(row), lanes(g)]
        for at in range(1, 16):
            total += plane_in[at, :, lanes(g)]
        plane_sum[:, lanes(g)] = total
        return [
            send(
                plane_sum.at[:, lanes(g)],
                line_in.at[NZ - dz, :, lanes(g)],
                gram_sems,
                g * 40 + 16 + NZ - dz,
                device(dz=dz),
            )
            for dz in LINE
        ]

    def over_line(g, copies):
        for copy in copies:
            copy.wait_recv()
        total = plane_sum[:, lanes(g)]
        for at in range(1, NZ):
            total += line_in[at, :, lanes(g)]
        line_sum[:, lanes(g)] = total
        gram_half[core, slice_at(row), lanes(g)] = total
        return [
            send(
                line_sum.at[:, lanes(g)],
                gram_half.at[core, slice_at(row), lanes(g)],
                gram_sems,
                g * 40 + 24 + (-dy % NY) * NX + (-dx % NX),
                device(dy=dy, dx=dx),
            )
            for dy, dx in PLANE
        ]

    def to_other(g, copies):
        for copy in copies:
            copy.wait_recv()
        half = gram_half.at[core, :, lanes(g)]
        return send(half, half, gram_sems, g * 40, other)

    work = {
        "share": share,
        "kernel": lambda a, b: kernel_rows(a * PTS, b * PTS),
        "first": first_product,
        "second": second_product,
        "third": lambda p: pair_product(p, 3, 5),
        "fourth": lambda p: pair_product(p, 5, 7),
        "last": lambda p: pair_product(p, 7, 8),
        "pass": pass_on,
        "finish": finish,
    }
    for name, *which in ORDER:
        work[name](*which)
    for copy in basis_copies:
        copy.wait_recv()
    early = chip_blocks(0)
    finish(3)
    basis_copies[3].wait_recv()
    late = chip_blocks(1)
    early = over_plane(0, early)
    late = over_plane(1, late)
    early = over_line(0, early)
    late = over_line(1, late)
    early = to_other(0, early)
    late = to_other(1, late)
    early.wait_recv()
    late.wait_recv()

    norm_square = jnp.zeros((8, 128), jnp.float32)
    for k in range(NCORE):
        for b, (i, j) in enumerate(BLOCKS[k]):
            block = gram_half[k, :, b * 128 : (b + 1) * 128]
            gram[i * 128 : i * 128 + 128, j * 128 : j * 128 + 128] = block
            if i != j:
                gram[j * 128 : j * 128 + 128, i * 128 : i * 128 + 128] = block.T
            squares = jnp.sum((block * block).reshape(16, 8, 128), axis=0)
            norm_square += squares if i == j else 2.0 * squares
    scale = jnp.sqrt(jnp.sum(jnp.sum(norm_square, axis=0, keepdims=True), axis=1, keepdims=True))

    def dot(a, b):
        return jnp.dot(
            a, b, precision=lax.Precision.HIGH, preferred_element_type=jnp.float32
        )

    gram[...] = gram[...] * (1.0 / scale)
    square[...] = dot(gram[...], gram[...])
    inner = 0.0625 * square[...] - 0.5625 * gram[...]
    unit = (
        lax.broadcasted_iota(jnp.int32, (RANK, RANK), 0)
        == lax.broadcasted_iota(jnp.int32, (RANK, RANK), 1)
    ).astype(jnp.float32)
    polynomial[...] = (
        dot(square[...], inner + 1.6875 * unit) - 2.4375 * gram[...] + 2.25 * unit
    )
    start = dot(basis[0], polynomial[...])
    step = dot(start, gram[...])
    step = dot(step, polynomial[...])
    step = dot(step, polynomial[...])
    out[...] = (1.5 * start - 0.5 * step) * (math.sqrt(RANK) * lax.rsqrt(scale))

    for copy in started:
        copy.wait_send()


def per_device(points, amplitude, sketch):
    f32, bf16 = jnp.float32, jnp.bfloat16
    vmem = pl.BlockSpec(memory_space=pltpu.VMEM)
    return pl.pallas_call(
        kernel,
        out_shape=jax.ShapeDtypeStruct((PTS, RANK), f32),
        in_specs=[vmem] * 3,
        out_specs=vmem,
        scratch_shapes=[
            pltpu.VMEM((8, PTS), f32),
            pltpu.VMEM((8, PTS), f32),
            pltpu.VMEM((NZ, 8, PTS), f32),
            pltpu.VMEM((NCORE, NY, NX, 8, PTS), f32),
            pltpu.VMEM((ROWS, 128), bf16),
            pltpu.VMEM((ROWS, 128), f32),
            pltpu.VMEM((128, COLS), bf16),
            pltpu.VMEM((8, COLS), f32),
            pltpu.VMEM((ROWS, COLS), bf16),
            pltpu.VMEM((PARTS, NCORE, NY, NX, PTS, WIDTH), bf16),
            pltpu.VMEM((PARTS, NZ, PTS, WIDTH), f32),
            pltpu.VMEM((PARTS, 7, HALF, WIDTH), f32),
            pltpu.VMEM((PARTS, 7, HALF, WIDTH), f32),
            pltpu.VMEM((NCORE, PTS, RANK), f32),
            pltpu.VMEM((128, 640), f32),
            pltpu.VMEM((16, 8, 640), f32),
            pltpu.VMEM((8, 640), f32),
            pltpu.VMEM((NZ, 8, 640), f32),
            pltpu.VMEM((8, 640), f32),
            pltpu.VMEM((NCORE, 128, 640), f32),
            pltpu.VMEM((RANK, RANK), f32),
            pltpu.VMEM((RANK, RANK), f32),
            pltpu.VMEM((RANK, RANK), f32),
            pltpu.SemaphoreType.DMA((2, 24)),
            pltpu.SemaphoreType.DMA((2, 16 * PARTS)),
            pltpu.SemaphoreType.DMA((2, 14 * PARTS)),
            pltpu.SemaphoreType.DMA((2, PARTS)),
            pltpu.SemaphoreType.DMA((2, 80)),
            pltpu.SemaphoreType.REGULAR,
        ],
        compiler_params=pltpu.CompilerParams(
            collective_id=0, has_side_effects=True, vmem_limit_bytes=28 << 20
        ),
        cost_estimate=pl.CostEstimate(
            flops=7_000_000_000, bytes_accessed=1 << 20, transcendentals=8 << 20
        ),
        name="kl_modes",
    )(points, amplitude.reshape(1, -1), sketch)


def solution(mesh):
    in_specs = (P(None, ("row", "col")), P(("row", "col")), P(("row", "col"), None))
    out_specs = P(("row", "col"), None)
    return jax.shard_map(
        per_device, mesh=mesh, in_specs=in_specs, out_specs=out_specs, check_vma=False
    )
```

```python
import math

import jax
import jax.numpy as jnp
from jax import lax
from jax.experimental import pallas as pl
from jax.experimental.pallas import tpu as pltpu
from jax.sharding import PartitionSpec as P

NS_ITERS = 3
CORRELATION = 4.0

MESH = pl.DeviceIdType.MESH
NX, NY, NZ, NCORE = 4, 4, 8, 2
PTS = 128
RANK = 512
WIDTH = 128
PARTS = RANK // WIDTH
HALF = PTS // 2
LANES = 1024
ROWS = NZ * PTS
COLS = NX * NY * NCORE * PTS
FEATS = 48
OFFSETS = (4, 3, -3, 2, -2, 1, -1, 0)
SLOT = {off: i for i, off in enumerate(OFFSETS)}
UP = ((4, 0), (3, 1), (3, 0), (2, 1), (2, 0), (1, 1), (1, 0))
DOWN = ((4, 1), (-3, 0), (-3, 1), (-2, 0), (-2, 1), (-1, 0), (-1, 1))
BLOCKS = (
    ((0, 0), (0, 1), (1, 1), (0, 3), (1, 3)),
    ((0, 2), (1, 2), (2, 2), (2, 3), (3, 3)),
)
GROUPS = ((0, 3), (3, 5))
ORDER = (
    ("kernel", 0, 1), ("share", 0), ("share", 1), ("kernel", 1, 3), ("first", 0), ("first", 1),
    ("share", 2), ("second", 0), ("second", 1), ("first", 2), ("second", 2), ("kernel", 3, 5),
    ("pass", 1, 2), ("share", 3), ("pass", 0, 2), ("third", 0), ("pass", 0, 3), ("pass", 1, 3),
    ("first", 3), ("pass", 2, 2), ("second", 3), ("kernel", 5, 7), ("pass", 0, 4), ("pass", 1, 4),
    ("fourth", 0), ("pass", 1, 5), ("pass", 0, 5), ("pass", 3, 2), ("third", 1), ("pass", 2, 3),
    ("pass", 2, 4), ("pass", 3, 3), ("fourth", 1), ("pass", 0, 6), ("last", 1), ("pass", 1, 6),
    ("last", 0), ("pass", 3, 4), ("pass", 2, 5), ("pass", 2, 6), ("pass", 3, 5), ("finish", 0),
    ("finish", 1), ("pass", 3, 6), ("finish", 2),
)
PLANE = tuple(
    sorted(
        ((dy, dx) for dy in range(NY) for dx in range(NX) if (dy, dx) != (0, 0)),
        key=lambda p: -(min(p[0], NY - p[0]) + min(p[1], NX - p[1])),
    )
)
LINE = tuple(sorted(range(1, NZ), key=lambda d: -min(d, NZ - d)))


def three_parts(v):
    high = v.astype(jnp.bfloat16).astype(jnp.float32)
    rest = v - high
    mid = rest.astype(jnp.bfloat16).astype(jnp.float32)
    low = (rest - mid).astype(jnp.bfloat16).astype(jnp.float32)
    return high, mid, low


def kernel(
    points,
    amplitude,
    sketch,
    out,
    row_pack,
    col_pack,
    row_packs,
    col_packs,
    row_feats,
    row_level,
    col_feats,
    col_level,
    tile,
    stripe,
    partial,
    up_in,
    down_in,
    basis,
    gram_part,
    plane_in,
    plane_sum,
    line_in,
    line_sum,
    gram_half,
    gram,
    square,
    polynomial,
    pack_sems,
    stripe_sems,
    ring_sems,
    basis_sems,
    gram_sems,
    ready,
):
    row = lax.axis_index("row")
    col = lax.axis_index("col")
    y, x = lax.div(row, NX), lax.rem(row, NX)
    z, core = lax.div(col, NCORE), lax.rem(col, NCORE)

    def device(dy=0, dx=0, dz=0, dcore=0):
        return (
            lax.rem(y + dy + NY, NY) * NX + lax.rem(x + dx + NX, NX),
            lax.rem(z + dz + NZ, NZ) * NCORE + lax.rem(core + dcore + NCORE, NCORE),
        )

    def send(src, dst, sems, index, to):
        copy = pltpu.make_async_remote_copy(
            src_ref=src,
            dst_ref=dst,
            send_sem=sems.at[0, index],
            recv_sem=sems.at[1, index],
            device_id=to,
            device_id_type=MESH,
        )
        copy.start()
        started.append(copy)
        return copy

    started = []
    other = device(dcore=1)

    barrier = pltpu.get_barrier_semaphore()

    def report(to_core, **where):
        pl.semaphore_signal(
            barrier, inc=1, device_id=device(dcore=to_core - core, **where), device_id_type=MESH
        )

    for dz in LINE:
        report(1, dz=dz)
    for d in range(1, 4):
        report(0, dx=d)
        report(0, dy=d)
    pl.semaphore_signal(barrier, inc=1, device_id=other, device_id_type=MESH)

    weight = 0.5 / math.sqrt(ROWS * NX * NY * NCORE)
    per_unit = 1.0 / (CORRELATION * math.log(2.0))
    amp = amplitude[...]
    level = jnp.log(amp) * (1.0 / math.log(2.0)) + 0.5 * math.log2(weight)
    ux = (points[0:1, :] - 0.5) * per_unit
    uy = (points[1:2, :] - 0.5) * per_unit
    uz = (points[2:3, :] - 4.0) * per_unit
    norm = ux * ux + uy * uy + uz * uz
    row_pack[...] = jnp.zeros_like(row_pack)
    col_pack[...] = jnp.zeros_like(col_pack)
    for i, v in enumerate((ux, uy, uz)):
        row_pack[i : i + 1, :] = v
        col_pack[i : i + 1, :] = -2.0 * v
    row_pack[3:4, :] = norm
    row_pack[4:5, :] = jnp.ones_like(norm)
    row_pack[5:6, :] = level
    col_pack[3:4, :] = jnp.ones_like(norm)
    col_pack[4:5, :] = norm
    col_pack[6:7, :] = level
    row_packs[SLOT[0]] = row_pack[...]
    col_packs[0, 0, 0] = col_pack[...]
    for t in range(4):
        stripe[t, 0, 0, 0] = sketch[:, t * 128 : (t + 1) * 128]

    @pl.when(core == 0)
    def _():
        pl.semaphore_wait(barrier, 13)
        pl.semaphore_signal(ready, inc=1, device_id=other, device_id_type=MESH)

    @pl.when(core == 1)
    def _():
        pl.semaphore_wait(ready, 1)

    near, far = slice(0, HALF), slice(HALF, PTS)

    def first_stage(t):
        copies = []
        where = slice(t * WIDTH, (t + 1) * WIDTH)
        for d in range(1, 4):
            copies.append(
                send(
                    sketch.at[near, where],
                    stripe.at[t, 0, 0, -d % NX, near],
                    stripe_sems,
                    t * 16 + d,
                    device(dx=d),
                )
            )
            copies.append(
                send(
                    sketch.at[far, where],
                    stripe.at[t, 0, -d % NY, 0, far],
                    stripe_sems,
                    t * 16 + 3 + d,
                    device(dy=d),
                )
            )
        return copies

    def second_stage(t):
        for copy in first[t]:
            copy.wait_recv()
        copies = []
        for d in range(1, 4):
            copies.append(
                send(
                    stripe.at[t, 0, 0, :, near],
                    stripe.at[t, 0, -d % NY, :, near],
                    stripe_sems,
                    t * 16 + 6 + d,
                    device(dy=d),
                )
            )
            copies.append(
                send(
                    stripe.at[t, 0, :, 0, far],
                    stripe.at[t, 0, :, -d % NX, far],
                    stripe_sems,
                    t * 16 + 9 + d,
                    device(dx=d),
                )
            )
        return copies

    packs_x = [
        send(col_pack, col_packs.at[0, 0, -d % NX], pack_sems, 8 + d, device(dx=d))
        for d in range(1, 4)
    ]
    first = {t: first_stage(t) for t in range(PARTS)}

    @pl.when(core == 1)
    def _():
        pl.semaphore_wait(barrier, 15)
        pl.semaphore_signal(ready, inc=1, device_id=other, device_id_type=MESH)

    @pl.when(core == 0)
    def _():
        pl.semaphore_wait(ready, 1)

    line_packs = []
    for dz in LINE:
        at = SLOT[-dz if dz <= 3 else 8 - dz]
        line_packs.append(send(row_pack, row_packs.at[at], pack_sems, at, device(dz=dz)))
    for copy in packs_x:
        copy.wait_recv()
    packs_y = [
        send(col_packs.at[0, 0], col_packs.at[0, -d % NY], pack_sems, 11 + d, device(dy=d))
        for d in range(1, 4)
    ]
    second = {t: second_stage(t) for t in range(PARTS)}
    for copy in packs_y:
        copy.wait_recv()
    pack_share = send(col_packs.at[0], col_packs.at[1], pack_sems, 8, other)

    def row_side(i, carry):
        pack = row_packs[i]
        high, mid, low = three_parts(pack)
        feats = jnp.concatenate([high, high, mid, high, low, mid], axis=0)
        feats = jnp.concatenate([feats, jnp.zeros((128 - FEATS, PTS), jnp.float32)], axis=0)
        at = pl.multiple_of(i * PTS, PTS)
        row_feats[pl.ds(at, PTS), :] = feats.T.astype(jnp.bfloat16)
        row_level[pl.ds(at, PTS), :] = jnp.broadcast_to(pack[5:6, :], (PTS, PTS)).T
        return carry

    def column_side(k):
        for dy in range(NY):
            for dx in range(NX):
                pack = col_packs[k, dy, dx]
                high, mid, low = three_parts(pack)
                feats = jnp.concatenate([high, mid, high, low, high, mid], axis=0)
                at = ((k * NY + dy) * NX + dx) * PTS
                col_feats[0:FEATS, at : at + PTS] = feats.astype(jnp.bfloat16)
                col_level[0:1, at : at + PTS] = pack[6:7, :]

    col_feats[FEATS:, :] = jnp.zeros((128 - FEATS, COLS), jnp.bfloat16)
    column_side(0)
    pack_share.wait_recv()
    column_side(1)
    row_side(SLOT[0], 0)

    def kernel_rows(start, stop):
        def body(i, carry):
            at = pl.multiple_of(i * LANES, LANES)
            feats = col_feats[:, pl.ds(at, LANES)]
            level = col_level[0:1, pl.ds(at, LANES)]
            for m in range(start, stop, PTS):
                distance = jnp.dot(
                    row_feats[m : m + PTS, :], feats, preferred_element_type=jnp.float32
                )
                distance = jnp.maximum(distance, 1e-30)
                root = distance * lax.rsqrt(distance)
                levels = jnp.concatenate([row_level[m : m + PTS, :]] * (LANES // PTS), axis=1)
                tile[m : m + PTS, pl.ds(at, LANES)] = jnp.exp2(levels + level - root).astype(
                    jnp.bfloat16
                )
            return carry

        lax.fori_loop(0, COLS // LANES, body, 0)

    def place_diagonal():
        own = slice(SLOT[0] * PTS, SLOT[0] * PTS + PTS)
        on_diagonal = lax.broadcasted_iota(jnp.int32, (PTS, PTS), 0) == lax.broadcasted_iota(
            jnp.int32, (PTS, PTS), 1
        )
        diagonal = jnp.broadcast_to(weight * amp * amp + 1.0, (PTS, PTS))
        tile[own, 0:PTS] = jnp.where(
            on_diagonal, diagonal, tile[own, 0:PTS].astype(jnp.float32)
        ).astype(jnp.bfloat16)

    kernel_rows(SLOT[0] * PTS, NZ * PTS)
    place_diagonal()
    for copy in line_packs:
        copy.wait_recv()
    lax.fori_loop(0, SLOT[0], row_side, 0)

    up, down, shares = {}, {}, {}

    def share(c):
        for copy in second[c]:
            copy.wait_recv()
        shares[c] = send(stripe.at[c, 0], stripe.at[c, 1], stripe_sems, c * 16, other)

    def block_product(c, start, stop):
        partial[c, start:stop] = jnp.dot(
            tile[start * PTS : stop * PTS, :],
            stripe[c].reshape(COLS, WIDTH),
            preferred_element_type=jnp.float32,
        ).reshape(stop - start, PTS, WIDTH)

    def pair_product(p, start, stop):
        chunks = (2 * p, 2 * p + 1)
        value = jnp.dot(
            tile[start * PTS : stop * PTS, :],
            jnp.concatenate([stripe[c].reshape(COLS, WIDTH) for c in chunks], axis=1),
            preferred_element_type=jnp.float32,
        )
        for i, c in enumerate(chunks):
            partial[c, start:stop] = value[:, i * WIDTH : (i + 1) * WIDTH].reshape(
                stop - start, PTS, WIDTH
            )

    def half_of(c, off, half):
        return partial.at[c, SLOT[off], half * HALF : (half + 1) * HALF]

    def pass_on(c, *steps):
        for i in steps:
            for sends, plan, arrived, dz, base in (
                (up, UP, up_in, 1, 0),
                (down, DOWN, down_in, -1, 7),
            ):
                off, half = plan[i]
                mine = half_of(c, off, half)
                if i >= 2:
                    sends[c, i - 2].wait_recv()
                    mine[...] += arrived[c, i - 2]
                sends[c, i] = send(
                    mine, arrived.at[c, i], ring_sems, c * 14 + base + i, device(dz=dz)
                )

    def first_product(c):
        shares[c].wait_recv()
        block_product(c, 0, 1)
        pass_on(c, 0)

    def second_product(c):
        block_product(c, 1, 3)
        pass_on(c, 1)

    basis_copies = []

    def finish(c):
        for i, (a, b) in ((5, (1, 0)), (6, (0, 1))):
            up[c, i].wait_recv()
            half_of(c, 0, a)[...] += up_in[c, i]
            down[c, i].wait_recv()
            half_of(c, 0, b)[...] += down_in[c, i]
        where = slice(c * WIDTH, (c + 1) * WIDTH)
        basis[0, :, where] = partial[c, SLOT[0]]
        basis_copies.append(
            send(basis.at[0, :, where], basis.at[1, :, where], basis_sems, c, other)
        )

    def columns(i):
        at = pl.multiple_of(i * 128, 128)
        return jnp.concatenate([basis[0, :, pl.ds(at, 128)], basis[1, :, pl.ds(at, 128)]], axis=0)

    def slice_at(r):
        return pl.ds(pl.multiple_of(r * 8, 8), 8)

    def lanes(g):
        return slice(GROUPS[g][0] * 128, GROUPS[g][1] * 128)

    def chip_blocks(g):
        for b in range(*GROUPS[g]):
            (i0, j0), (i1, j1) = BLOCKS[0][b], BLOCKS[1][b]
            gram_part[:, b * 128 : (b + 1) * 128] = lax.dot_general(
                columns(i0 + core * (i1 - i0)),
                columns(j0 + core * (j1 - j0)),
                (((0,), (0,)), ((), ())),
                precision=lax.Precision.HIGH,
                preferred_element_type=jnp.float32,
            )
        copies = []
        for dy, dx in PLANE:
            to = device(dy=dy, dx=dx)
            at = (-dy % NY) * NX + (-dx % NX)
            copies.append(
                send(
                    gram_part.at[slice_at(to[0]), lanes(g)],
                    plane_in.at[at, :, lanes(g)],
                    gram_sems,
                    g * 40 + at,
                    to,
                )
            )
        return copies

    def over_plane(g, copies):
        for copy in copies:
            copy.wait_recv()
        total = gram_part[slice_at(row), lanes(g)]
        for at in range(1, 16):
            total += plane_in[at, :, lanes(g)]
        plane_sum[:, lanes(g)] = total
        return [
            send(
                plane_sum.at[:, lanes(g)],
                line_in.at[NZ - dz, :, lanes(g)],
                gram_sems,
                g * 40 + 16 + NZ - dz,
                device(dz=dz),
            )
            for dz in LINE
        ]

    def over_line(g, copies):
        for copy in copies:
            copy.wait_recv()
        total = plane_sum[:, lanes(g)]
        for at in range(1, NZ):
            total += line_in[at, :, lanes(g)]
        line_sum[:, lanes(g)] = total
        gram_half[core, slice_at(row), lanes(g)] = total
        return [
            send(
                line_sum.at[:, lanes(g)],
                gram_half.at[core, slice_at(row), lanes(g)],
                gram_sems,
                g * 40 + 24 + (-dy % NY) * NX + (-dx % NX),
                device(dy=dy, dx=dx),
            )
            for dy, dx in PLANE
        ]

    def to_other(g, copies):
        for copy in copies:
            copy.wait_recv()
        half = gram_half.at[core, :, lanes(g)]
        return send(half, half, gram_sems, g * 40, other)

    work = {
        "share": share,
        "kernel": lambda a, b: kernel_rows(a * PTS, b * PTS),
        "first": first_product,
        "second": second_product,
        "third": lambda p: pair_product(p, 3, 5),
        "fourth": lambda p: pair_product(p, 5, 7),
        "last": lambda p: pair_product(p, 7, 8),
        "pass": pass_on,
        "finish": finish,
    }
    for name, *which in ORDER:
        work[name](*which)
    for copy in basis_copies:
        copy.wait_recv()
    def drain(count):
        for copy in started[:count]:
            copy.wait_send()
        del started[:count]

    ring_sends = len(started)
    early = chip_blocks(0)
    finish(3)
    basis_copies[3].wait_recv()
    late = chip_blocks(1)
    block_sends = len(started) - ring_sends
    drain(ring_sends)
    early = over_plane(0, early)
    late = over_plane(1, late)
    drain(block_sends)
    line_sends = len(started)
    early = over_line(0, early)
    late = over_line(1, late)
    drain(line_sends)
    plane_sends = len(started)
    early = to_other(0, early)
    late = to_other(1, late)
    drain(plane_sends)
    early.wait_recv()
    late.wait_recv()

    norm_square = jnp.zeros((8, 128), jnp.float32)
    for k in range(NCORE):
        for b, (i, j) in enumerate(BLOCKS[k]):
            block = gram_half[k, :, b * 128 : (b + 1) * 128]
            gram[i * 128 : i * 128 + 128, j * 128 : j * 128 + 128] = block
            if i != j:
                gram[j * 128 : j * 128 + 128, i * 128 : i * 128 + 128] = block.T
            squares = jnp.sum((block * block).reshape(16, 8, 128), axis=0)
            norm_square += squares if i == j else 2.0 * squares
    scale = jnp.sqrt(jnp.sum(jnp.sum(norm_square, axis=0, keepdims=True), axis=1, keepdims=True))

    def dot(a, b):
        return jnp.dot(
            a, b, precision=lax.Precision.HIGH, preferred_element_type=jnp.float32
        )

    gram[...] = gram[...] * (1.0 / scale)
    square[...] = dot(gram[...], gram[...])
    inner = 0.0625 * square[...] - 0.5625 * gram[...]
    unit = (
        lax.broadcasted_iota(jnp.int32, (RANK, RANK), 0)
        == lax.broadcasted_iota(jnp.int32, (RANK, RANK), 1)
    ).astype(jnp.float32)
    polynomial[...] = (
        dot(square[...], inner + 1.6875 * unit) - 2.4375 * gram[...] + 2.25 * unit
    )
    start = dot(basis[0], polynomial[...])
    step = dot(start, gram[...])
    step = dot(step, polynomial[...])
    step = dot(step, polynomial[...])
    out[...] = (1.5 * start - 0.5 * step) * (math.sqrt(RANK) * lax.rsqrt(scale))

    drain(len(started))


def per_device(points, amplitude, sketch):
    f32, bf16 = jnp.float32, jnp.bfloat16
    vmem = pl.BlockSpec(memory_space=pltpu.VMEM)
    return pl.pallas_call(
        kernel,
        out_shape=jax.ShapeDtypeStruct((PTS, RANK), f32),
        in_specs=[vmem] * 3,
        out_specs=vmem,
        scratch_shapes=[
            pltpu.VMEM((8, PTS), f32),
            pltpu.VMEM((8, PTS), f32),
            pltpu.VMEM((NZ, 8, PTS), f32),
            pltpu.VMEM((NCORE, NY, NX, 8, PTS), f32),
            pltpu.VMEM((ROWS, 128), bf16),
            pltpu.VMEM((ROWS, 128), f32),
            pltpu.VMEM((128, COLS), bf16),
            pltpu.VMEM((8, COLS), f32),
            pltpu.VMEM((ROWS, COLS), bf16),
            pltpu.VMEM((PARTS, NCORE, NY, NX, PTS, WIDTH), bf16),
            pltpu.VMEM((PARTS, NZ, PTS, WIDTH), f32),
            pltpu.VMEM((PARTS, 7, HALF, WIDTH), f32),
            pltpu.VMEM((PARTS, 7, HALF, WIDTH), f32),
            pltpu.VMEM((NCORE, PTS, RANK), f32),
            pltpu.VMEM((128, 640), f32),
            pltpu.VMEM((16, 8, 640), f32),
            pltpu.VMEM((8, 640), f32),
            pltpu.VMEM((NZ, 8, 640), f32),
            pltpu.VMEM((8, 640), f32),
            pltpu.VMEM((NCORE, 128, 640), f32),
            pltpu.VMEM((RANK, RANK), f32),
            pltpu.VMEM((RANK, RANK), f32),
            pltpu.VMEM((RANK, RANK), f32),
            pltpu.SemaphoreType.DMA((2, 24)),
            pltpu.SemaphoreType.DMA((2, 16 * PARTS)),
            pltpu.SemaphoreType.DMA((2, 14 * PARTS)),
            pltpu.SemaphoreType.DMA((2, PARTS)),
            pltpu.SemaphoreType.DMA((2, 80)),
            pltpu.SemaphoreType.REGULAR,
        ],
        compiler_params=pltpu.CompilerParams(
            collective_id=0, has_side_effects=True, vmem_limit_bytes=28 << 20
        ),
        cost_estimate=pl.CostEstimate(
            flops=7_000_000_000, bytes_accessed=1 << 20, transcendentals=8 << 20
        ),
        name="kl_modes",
    )(points, amplitude.reshape(1, -1), sketch)


def solution(mesh):
    in_specs = (P(None, ("row", "col")), P(("row", "col")), P(("row", "col"), None))
    out_specs = P(("row", "col"), None)
    return jax.shard_map(
        per_device, mesh=mesh, in_specs=in_specs, out_specs=out_specs, check_vma=False
    )
```

```python
import math

import jax
import jax.numpy as jnp
from jax import lax
from jax.experimental import pallas as pl
from jax.experimental.pallas import tpu as pltpu
from jax.sharding import PartitionSpec as P

NS_ITERS = 3
CORRELATION = 4.0

MESH = pl.DeviceIdType.MESH
NX, NY, NZ, NCORE = 4, 4, 8, 2
PTS = 128
RANK = 512
WIDTH = 128
PARTS = RANK // WIDTH
HALF = PTS // 2
LANES = 1024
ROWS = NZ * PTS
COLS = NX * NY * NCORE * PTS
FEATS = 48
OFFSETS = (4, 3, -3, 2, -2, 1, -1, 0)
SLOT = {off: i for i, off in enumerate(OFFSETS)}
UP = ((4, 0), (3, 1), (3, 0), (2, 1), (2, 0), (1, 1), (1, 0))
DOWN = ((4, 1), (-3, 0), (-3, 1), (-2, 0), (-2, 1), (-1, 0), (-1, 1))
BLOCKS = (
    ((0, 0), (0, 1), (1, 1), (0, 3), (1, 3)),
    ((0, 2), (1, 2), (2, 2), (2, 3), (3, 3)),
)
GROUPS = ((0, 3), (3, 5))
ORDER = (
    ("kernel", 0, 1), ("share", 0), ("share", 1), ("kernel", 1, 3), ("first", 0), ("first", 1),
    ("share", 2), ("second", 0), ("second", 1), ("first", 2), ("second", 2), ("kernel", 3, 5),
    ("pass", 1, 2), ("share", 3), ("pass", 0, 2), ("third", 0), ("pass", 0, 3), ("pass", 1, 3),
    ("first", 3), ("pass", 2, 2), ("second", 3), ("kernel", 5, 7), ("pass", 0, 4), ("pass", 1, 4),
    ("fourth", 0), ("pass", 1, 5), ("pass", 0, 5), ("pass", 3, 2), ("third", 1), ("pass", 2, 3),
    ("pass", 2, 4), ("pass", 3, 3), ("fourth", 1), ("pass", 0, 6), ("last", 1), ("pass", 1, 6),
    ("last", 0), ("pass", 3, 4), ("pass", 2, 5), ("pass", 2, 6), ("pass", 3, 5), ("finish", 0),
    ("finish", 1), ("pass", 3, 6), ("finish", 2),
)
PLANE = tuple(
    sorted(
        ((dy, dx) for dy in range(NY) for dx in range(NX) if (dy, dx) != (0, 0)),
        key=lambda p: -(min(p[0], NY - p[0]) + min(p[1], NX - p[1])),
    )
)
LINE = tuple(sorted(range(1, NZ), key=lambda d: -min(d, NZ - d)))


def three_parts(v):
    high = v.astype(jnp.bfloat16).astype(jnp.float32)
    rest = v - high
    mid = rest.astype(jnp.bfloat16).astype(jnp.float32)
    low = (rest - mid).astype(jnp.bfloat16).astype(jnp.float32)
    return high, mid, low


def kernel(
    points,
    amplitude,
    sketch,
    out,
    factor,
    row_pack,
    col_pack,
    row_packs,
    col_packs,
    row_feats,
    row_level,
    col_feats,
    col_level,
    tile,
    stripe,
    partial,
    up_in,
    down_in,
    basis,
    gram_part,
    plane_in,
    plane_sum,
    line_in,
    line_sum,
    gram_half,
    gram,
    square,
    polynomial,
    pack_sems,
    stripe_sems,
    ring_sems,
    basis_sems,
    gram_sems,
    ready,
):
    row = lax.axis_index("row")
    col = lax.axis_index("col")
    y, x = lax.div(row, NX), lax.rem(row, NX)
    z, core = lax.div(col, NCORE), lax.rem(col, NCORE)

    def device(dy=0, dx=0, dz=0, dcore=0):
        return (
            lax.rem(y + dy + NY, NY) * NX + lax.rem(x + dx + NX, NX),
            lax.rem(z + dz + NZ, NZ) * NCORE + lax.rem(core + dcore + NCORE, NCORE),
        )

    def send(src, dst, sems, index, to):
        copy = pltpu.make_async_remote_copy(
            src_ref=src,
            dst_ref=dst,
            send_sem=sems.at[0, index],
            recv_sem=sems.at[1, index],
            device_id=to,
            device_id_type=MESH,
        )
        copy.start()
        started.append(copy)
        return copy

    started = []
    other = device(dcore=1)

    barrier = pltpu.get_barrier_semaphore()

    def report(to_core, **where):
        pl.semaphore_signal(
            barrier, inc=1, device_id=device(dcore=to_core - core, **where), device_id_type=MESH
        )

    for dz in LINE:
        report(1, dz=dz)
    for d in range(1, 4):
        report(0, dx=d)
        report(0, dy=d)
    pl.semaphore_signal(barrier, inc=1, device_id=other, device_id_type=MESH)

    weight = 0.5 / math.sqrt(ROWS * NX * NY * NCORE)
    per_unit = 1.0 / (CORRELATION * math.log(2.0))
    amp = amplitude[...]
    level = jnp.log(amp) * (1.0 / math.log(2.0)) + 0.5 * math.log2(weight)
    ux = (points[0:1, :] - 0.5) * per_unit
    uy = (points[1:2, :] - 0.5) * per_unit
    uz = (points[2:3, :] - 4.0) * per_unit
    norm = ux * ux + uy * uy + uz * uz
    row_pack[...] = jnp.zeros_like(row_pack)
    col_pack[...] = jnp.zeros_like(col_pack)
    for i, v in enumerate((ux, uy, uz)):
        row_pack[i : i + 1, :] = v
        col_pack[i : i + 1, :] = -2.0 * v
    row_pack[3:4, :] = norm
    row_pack[4:5, :] = jnp.ones_like(norm)
    row_pack[5:6, :] = level
    col_pack[3:4, :] = jnp.ones_like(norm)
    col_pack[4:5, :] = norm
    col_pack[6:7, :] = level
    row_packs[SLOT[0]] = row_pack[...]
    col_packs[0, 0, 0] = col_pack[...]
    for t in range(4):
        stripe[t, 0, 0, 0] = sketch[:, t * 128 : (t + 1) * 128]

    @pl.when(core == 0)
    def _():
        pl.semaphore_wait(barrier, 13)
        pl.semaphore_signal(ready, inc=1, device_id=other, device_id_type=MESH)

    @pl.when(core == 1)
    def _():
        pl.semaphore_wait(ready, 1)

    near, far = slice(0, HALF), slice(HALF, PTS)

    def first_stage(t):
        copies = []
        where = slice(t * WIDTH, (t + 1) * WIDTH)
        for d in range(1, 4):
            copies.append(
                send(
                    sketch.at[near, where],
                    stripe.at[t, 0, 0, -d % NX, near],
                    stripe_sems,
                    t * 16 + d,
                    device(dx=d),
                )
            )
            copies.append(
                send(
                    sketch.at[far, where],
                    stripe.at[t, 0, -d % NY, 0, far],
                    stripe_sems,
                    t * 16 + 3 + d,
                    device(dy=d),
                )
            )
        return copies

    def second_stage(t):
        for copy in first[t]:
            copy.wait_recv()
        copies = []
        for d in range(1, 4):
            copies.append(
                send(
                    stripe.at[t, 0, 0, :, near],
                    stripe.at[t, 0, -d % NY, :, near],
                    stripe_sems,
                    t * 16 + 6 + d,
                    device(dy=d),
                )
            )
            copies.append(
                send(
                    stripe.at[t, 0, :, 0, far],
                    stripe.at[t, 0, :, -d % NX, far],
                    stripe_sems,
                    t * 16 + 9 + d,
                    device(dx=d),
                )
            )
        return copies

    packs_x = [
        send(col_pack, col_packs.at[0, 0, -d % NX], pack_sems, 8 + d, device(dx=d))
        for d in range(1, 4)
    ]
    first = {t: first_stage(t) for t in range(PARTS)}

    @pl.when(core == 1)
    def _():
        pl.semaphore_wait(barrier, 15)
        pl.semaphore_signal(ready, inc=1, device_id=other, device_id_type=MESH)

    @pl.when(core == 0)
    def _():
        pl.semaphore_wait(ready, 1)

    line_packs = []
    for dz in LINE:
        at = SLOT[-dz if dz <= 3 else 8 - dz]
        line_packs.append(send(row_pack, row_packs.at[at], pack_sems, at, device(dz=dz)))
    for copy in packs_x:
        copy.wait_recv()
    packs_y = [
        send(col_packs.at[0, 0], col_packs.at[0, -d % NY], pack_sems, 11 + d, device(dy=d))
        for d in range(1, 4)
    ]
    second = {t: second_stage(t) for t in range(PARTS)}
    for copy in packs_y:
        copy.wait_recv()
    pack_share = send(col_packs.at[0], col_packs.at[1], pack_sems, 8, other)

    def row_side(i, carry):
        pack = row_packs[i]
        high, mid, low = three_parts(pack)
        feats = jnp.concatenate([high, high, mid, high, low, mid], axis=0)
        feats = jnp.concatenate([feats, jnp.zeros((128 - FEATS, PTS), jnp.float32)], axis=0)
        at = pl.multiple_of(i * PTS, PTS)
        row_feats[pl.ds(at, PTS), :] = feats.T.astype(jnp.bfloat16)
        row_level[pl.ds(at, PTS), :] = jnp.broadcast_to(pack[5:6, :], (PTS, PTS)).T
        return carry

    def column_side(k):
        for dy in range(NY):
            for dx in range(NX):
                pack = col_packs[k, dy, dx]
                high, mid, low = three_parts(pack)
                feats = jnp.concatenate([high, mid, high, low, high, mid], axis=0)
                at = ((k * NY + dy) * NX + dx) * PTS
                col_feats[0:FEATS, at : at + PTS] = feats.astype(jnp.bfloat16)
                col_level[0:1, at : at + PTS] = pack[6:7, :]

    col_feats[FEATS:, :] = jnp.zeros((128 - FEATS, COLS), jnp.bfloat16)
    column_side(0)
    pack_share.wait_recv()
    column_side(1)
    row_side(SLOT[0], 0)

    def kernel_rows(start, stop):
        def body(i, carry):
            at = pl.multiple_of(i * LANES, LANES)
            feats = col_feats[:, pl.ds(at, LANES)]
            level = col_level[0:1, pl.ds(at, LANES)]
            for m in range(start, stop, PTS):
                distance = jnp.dot(
                    row_feats[m : m + PTS, :], feats, preferred_element_type=jnp.float32
                )
                distance = jnp.maximum(distance, 1e-30)
                root = distance * lax.rsqrt(distance)
                levels = jnp.concatenate([row_level[m : m + PTS, :]] * (LANES // PTS), axis=1)
                tile[m : m + PTS, pl.ds(at, LANES)] = jnp.exp2(levels + level - root).astype(
                    jnp.bfloat16
                )
            return carry

        lax.fori_loop(0, COLS // LANES, body, 0)

    def place_diagonal():
        own = slice(SLOT[0] * PTS, SLOT[0] * PTS + PTS)
        on_diagonal = lax.broadcasted_iota(jnp.int32, (PTS, PTS), 0) == lax.broadcasted_iota(
            jnp.int32, (PTS, PTS), 1
        )
        diagonal = jnp.broadcast_to(weight * amp * amp + 1.0, (PTS, PTS))
        tile[own, 0:PTS] = jnp.where(
            on_diagonal, diagonal, tile[own, 0:PTS].astype(jnp.float32)
        ).astype(jnp.bfloat16)

    kernel_rows(SLOT[0] * PTS, NZ * PTS)
    place_diagonal()
    for copy in line_packs:
        copy.wait_recv()
    lax.fori_loop(0, SLOT[0], row_side, 0)

    up, down, shares = {}, {}, {}

    def share(c):
        for copy in second[c]:
            copy.wait_recv()
        shares[c] = send(stripe.at[c, 0], stripe.at[c, 1], stripe_sems, c * 16, other)

    def block_product(c, start, stop):
        partial[c, start:stop] = jnp.dot(
            tile[start * PTS : stop * PTS, :],
            stripe[c].reshape(COLS, WIDTH),
            preferred_element_type=jnp.float32,
        ).reshape(stop - start, PTS, WIDTH)

    def pair_product(p, start, stop):
        chunks = (2 * p, 2 * p + 1)
        value = jnp.dot(
            tile[start * PTS : stop * PTS, :],
            jnp.concatenate([stripe[c].reshape(COLS, WIDTH) for c in chunks], axis=1),
            preferred_element_type=jnp.float32,
        )
        for i, c in enumerate(chunks):
            partial[c, start:stop] = value[:, i * WIDTH : (i + 1) * WIDTH].reshape(
                stop - start, PTS, WIDTH
            )

    def half_of(c, off, half):
        return partial.at[c, SLOT[off], half * HALF : (half + 1) * HALF]

    def pass_on(c, *steps):
        for i in steps:
            for sends, plan, arrived, dz, base in (
                (up, UP, up_in, 1, 0),
                (down, DOWN, down_in, -1, 7),
            ):
                off, half = plan[i]
                mine = half_of(c, off, half)
                if i >= 2:
                    sends[c, i - 2].wait_recv()
                    mine[...] += arrived[c, i - 2]
                sends[c, i] = send(
                    mine, arrived.at[c, i], ring_sems, c * 14 + base + i, device(dz=dz)
                )

    def first_product(c):
        shares[c].wait_recv()
        block_product(c, 0, 1)
        pass_on(c, 0)

    def second_product(c):
        block_product(c, 1, 3)
        pass_on(c, 1)

    basis_copies = []

    def finish(c):
        for i, (a, b) in ((5, (1, 0)), (6, (0, 1))):
            up[c, i].wait_recv()
            half_of(c, 0, a)[...] += up_in[c, i]
            down[c, i].wait_recv()
            half_of(c, 0, b)[...] += down_in[c, i]
        where = slice(c * WIDTH, (c + 1) * WIDTH)
        basis[0, :, where] = partial[c, SLOT[0]]
        basis_copies.append(
            send(basis.at[0, :, where], basis.at[1, :, where], basis_sems, c, other)
        )

    def columns(i):
        at = pl.multiple_of(i * 128, 128)
        return jnp.concatenate([basis[0, :, pl.ds(at, 128)], basis[1, :, pl.ds(at, 128)]], axis=0)

    def slice_at(r):
        return pl.ds(pl.multiple_of(r * 8, 8), 8)

    def lanes(g):
        return slice(GROUPS[g][0] * 128, GROUPS[g][1] * 128)

    def chip_blocks(g):
        for b in range(*GROUPS[g]):
            (i0, j0), (i1, j1) = BLOCKS[0][b], BLOCKS[1][b]
            gram_part[:, b * 128 : (b + 1) * 128] = lax.dot_general(
                columns(i0 + core * (i1 - i0)),
                columns(j0 + core * (j1 - j0)),
                (((0,), (0,)), ((), ())),
                precision=lax.Precision.HIGH,
                preferred_element_type=jnp.float32,
            )
        copies = []
        for dy, dx in PLANE:
            to = device(dy=dy, dx=dx)
            at = (-dy % NY) * NX + (-dx % NX)
            copies.append(
                send(
                    gram_part.at[slice_at(to[0]), lanes(g)],
                    plane_in.at[at, :, lanes(g)],
                    gram_sems,
                    g * 40 + at,
                    to,
                )
            )
        return copies

    def over_plane(g, copies):
        for copy in copies:
            copy.wait_recv()
        total = gram_part[slice_at(row), lanes(g)]
        for at in range(1, 16):
            total += plane_in[at, :, lanes(g)]
        plane_sum[:, lanes(g)] = total
        return [
            send(
                plane_sum.at[:, lanes(g)],
                line_in.at[NZ - dz, :, lanes(g)],
                gram_sems,
                g * 40 + 16 + NZ - dz,
                device(dz=dz),
            )
            for dz in LINE
        ]

    def over_line(g, copies):
        for copy in copies:
            copy.wait_recv()
        total = plane_sum[:, lanes(g)]
        for at in range(1, NZ):
            total += line_in[at, :, lanes(g)]
        line_sum[:, lanes(g)] = total
        gram_half[core, slice_at(row), lanes(g)] = total
        return [
            send(
                line_sum.at[:, lanes(g)],
                gram_half.at[core, slice_at(row), lanes(g)],
                gram_sems,
                g * 40 + 24 + (-dy % NY) * NX + (-dx % NX),
                device(dy=dy, dx=dx),
            )
            for dy, dx in PLANE
        ]

    def to_other(g, copies):
        for copy in copies:
            copy.wait_recv()
        half = gram_half.at[core, :, lanes(g)]
        return send(half, half, gram_sems, g * 40, other)

    work = {
        "share": share,
        "kernel": lambda a, b: kernel_rows(a * PTS, b * PTS),
        "first": first_product,
        "second": second_product,
        "third": lambda p: pair_product(p, 3, 5),
        "fourth": lambda p: pair_product(p, 5, 7),
        "last": lambda p: pair_product(p, 7, 8),
        "pass": pass_on,
        "finish": finish,
    }
    for name, *which in ORDER:
        work[name](*which)
    for copy in basis_copies:
        copy.wait_recv()
    def drain(count):
        for copy in started[:count]:
            copy.wait_send()
        del started[:count]

    ring_sends = len(started)
    early = chip_blocks(0)
    finish(3)
    basis_copies[3].wait_recv()
    late = chip_blocks(1)
    block_sends = len(started) - ring_sends
    drain(ring_sends)
    early = over_plane(0, early)
    late = over_plane(1, late)
    drain(block_sends)
    line_sends = len(started)
    early = over_line(0, early)
    late = over_line(1, late)
    drain(line_sends)
    plane_sends = len(started)
    early = to_other(0, early)
    late = to_other(1, late)
    drain(plane_sends)
    early.wait_recv()
    late.wait_recv()

    norm_square = jnp.zeros((8, 128), jnp.float32)
    for k in range(NCORE):
        for b, (i, j) in enumerate(BLOCKS[k]):
            block = gram_half[k, :, b * 128 : (b + 1) * 128]
            gram[i * 128 : i * 128 + 128, j * 128 : j * 128 + 128] = block
            if i != j:
                gram[j * 128 : j * 128 + 128, i * 128 : i * 128 + 128] = block.T
            squares = jnp.sum((block * block).reshape(16, 8, 128), axis=0)
            norm_square += squares if i == j else 2.0 * squares
    scale = jnp.sqrt(jnp.sum(jnp.sum(norm_square, axis=0, keepdims=True), axis=1, keepdims=True))

    def dot(a, b):
        return jnp.dot(
            a, b, precision=lax.Precision.HIGH, preferred_element_type=jnp.float32
        )

    gram[...] = gram[...] * (1.0 / scale)
    square[...] = dot(gram[...], gram[...])
    inner = 0.0625 * square[...] - 0.5625 * gram[...]
    unit = (
        lax.broadcasted_iota(jnp.int32, (RANK, RANK), 0)
        == lax.broadcasted_iota(jnp.int32, (RANK, RANK), 1)
    ).astype(jnp.float32)
    polynomial[...] = (
        dot(square[...], inner + 1.6875 * unit) - 2.4375 * gram[...] + 2.25 * unit
    )
    start = dot(basis[0], polynomial[...])
    step = dot(start, gram[...])
    step = dot(step, polynomial[...])
    step = dot(step, polynomial[...])
    out[...] = 1.5 * start - 0.5 * step
    factor[...] = jnp.broadcast_to(math.sqrt(RANK) * lax.rsqrt(scale), (1, RANK))

    drain(len(started))


def per_device(points, amplitude, sketch):
    f32, bf16 = jnp.float32, jnp.bfloat16
    vmem = pl.BlockSpec(memory_space=pltpu.VMEM)
    modes, factor = pl.pallas_call(
        kernel,
        out_shape=[
            jax.ShapeDtypeStruct((PTS, RANK), f32),
            jax.ShapeDtypeStruct((1, RANK), f32),
        ],
        in_specs=[vmem] * 3,
        out_specs=[vmem] * 2,
        scratch_shapes=[
            pltpu.VMEM((8, PTS), f32),
            pltpu.VMEM((8, PTS), f32),
            pltpu.VMEM((NZ, 8, PTS), f32),
            pltpu.VMEM((NCORE, NY, NX, 8, PTS), f32),
            pltpu.VMEM((ROWS, 128), bf16),
            pltpu.VMEM((ROWS, 128), f32),
            pltpu.VMEM((128, COLS), bf16),
            pltpu.VMEM((8, COLS), f32),
            pltpu.VMEM((ROWS, COLS), bf16),
            pltpu.VMEM((PARTS, NCORE, NY, NX, PTS, WIDTH), bf16),
            pltpu.VMEM((PARTS, NZ, PTS, WIDTH), f32),
            pltpu.VMEM((PARTS, 7, HALF, WIDTH), f32),
            pltpu.VMEM((PARTS, 7, HALF, WIDTH), f32),
            pltpu.VMEM((NCORE, PTS, RANK), f32),
            pltpu.VMEM((128, 640), f32),
            pltpu.VMEM((16, 8, 640), f32),
            pltpu.VMEM((8, 640), f32),
            pltpu.VMEM((NZ, 8, 640), f32),
            pltpu.VMEM((8, 640), f32),
            pltpu.VMEM((NCORE, 128, 640), f32),
            pltpu.VMEM((RANK, RANK), f32),
            pltpu.VMEM((RANK, RANK), f32),
            pltpu.VMEM((RANK, RANK), f32),
            pltpu.SemaphoreType.DMA((2, 24)),
            pltpu.SemaphoreType.DMA((2, 16 * PARTS)),
            pltpu.SemaphoreType.DMA((2, 14 * PARTS)),
            pltpu.SemaphoreType.DMA((2, PARTS)),
            pltpu.SemaphoreType.DMA((2, 80)),
            pltpu.SemaphoreType.REGULAR,
        ],
        compiler_params=pltpu.CompilerParams(
            collective_id=0, has_side_effects=True, vmem_limit_bytes=28 << 20
        ),
        cost_estimate=pl.CostEstimate(
            flops=7_000_000_000, bytes_accessed=1 << 20, transcendentals=8 << 20
        ),
        name="kl_modes",
    )(points, amplitude.reshape(1, -1), sketch)
    return modes * factor


def solution(mesh):
    in_specs = (P(None, ("row", "col")), P(("row", "col")), P(("row", "col"), None))
    out_specs = P(("row", "col"), None)
    return jax.shard_map(
        per_device, mesh=mesh, in_specs=in_specs, out_specs=out_specs, check_vma=False
    )
```
